128 devices in a mesh: prow: 8 (over x, core), pcol: 16 (over z, y).
Axes of the slice: x: 4, y: 4, z: 4, core: 2. Of those that a mesh axis runs over, the one named last changes fastest.
Arguments:
- window: float32 [98304, 4096], P('prow', 'pcol'), as said below
- panel_index: int32 [1], replicated, may hold values from 0 to 15
Outputs:
- updated: float32 [98304, 4096], P('prow', 'pcol')
The draws below stay inside these ranges and needn't reach their ends.
Inputs may be any that keep to these rules, and one draw needn't show every extreme that they name: `window`: entries whose matrix row equals their matrix column lie in 32 to 64; all others are of order one.
All inputs are finite; a program needn't handle non-finite values.
Results may differ from the reference program's by a relative error of at most 0.0027.
Values may be sent and summed in bfloat16 or wider, within the bound.
No kernel may reach another device: no remote copies, remote signals or barrier semaphores. Data moves between devices by JAX's collectives and lax.ppermute only.
A program may use at most 128 MiB of HBM per device.

```python
import jax
import jax.numpy as jnp
from jax import lax

NB = 128
LOOK = 16
ROW_TILES = 96
ROWS = 98304
COLS = 4096
N_PROW = 8
N_PCOL = 16


def draw_window(key, part):
    key = jax.random.fold_in(key, 7)
    col_tiles = COLS // NB // N_PCOL
    stored_row = jnp.arange(ROWS)
    row_tile = stored_row // NB
    global_row = (row_tile % ROW_TILES * N_PROW + row_tile // ROW_TILES) * NB + stored_row % NB
    stored_col = jnp.arange(COLS)
    col_tile = stored_col // NB
    global_col = (col_tile % col_tiles * N_PCOL + col_tile // col_tiles) * NB + stored_col % NB
    first, second = jax.random.split(key, 2)
    noise = jax.random.normal(first, (ROWS, COLS), jnp.float32)
    diagonal = jax.random.uniform(second, (ROWS, COLS), jnp.float32, 32.0, 64.0)
    same = global_row[:, None] == global_col[None, :]
    return jnp.where(same, diagonal, noise)


def setup_inputs(seed: int = 0) -> dict:
    key_of = jax.random.split(jax.random.key(seed), 3)
    return {
        "window": draw_window(jax.random.fold_in(key_of[2], 71), 0),
        "panel_index": jax.random.randint(key_of[1], (1,), 0, N_PCOL).astype(jnp.int32),
    }


def reorder(matrix):
    col_tiles = COLS // NB // N_PCOL
    shaped = matrix.reshape(N_PROW, ROW_TILES, NB, N_PCOL, col_tiles, NB)
    return jnp.transpose(shaped, (1, 0, 2, 4, 3, 5)).reshape(matrix.shape)

def restore(matrix):
    col_tiles = COLS // NB // N_PCOL
    shaped = matrix.reshape(ROW_TILES, N_PROW, NB, col_tiles, N_PCOL, NB)
    return jnp.transpose(shaped, (1, 0, 2, 4, 3, 5)).reshape(matrix.shape)

def reference(window, panel_index):
    k = panel_index[0].astype(jnp.int32)
    whole = reorder(window)
    start = (k * NB).astype(jnp.int32)
    tile = lax.dynamic_slice(whole, (start, start), (NB, NB))
    factor = jnp.linalg.cholesky(tile)
    panel = lax.dynamic_slice_in_dim(whole, start, NB, 1)
    solved = jax.scipy.linalg.solve_triangular(factor, panel.T, lower=True).T
    low = solved.astype(jnp.bfloat16)
    row_tile = (jnp.arange(ROWS) // NB).astype(jnp.int32)
    placed = lax.dynamic_update_slice(jnp.zeros((ROWS, NB), jnp.float32), factor, (start, jnp.int32(0)))
    new_panel = jnp.where((row_tile > k)[:, None], solved, jnp.where((row_tile == k)[:, None], placed, panel))
    look_start = ((k + 1) * NB).astype(jnp.int32)
    look = lax.dynamic_slice_in_dim(low, look_start, LOOK * NB, 0)
    update = jnp.dot(low.astype(jnp.float32), look.T.astype(jnp.float32), preferred_element_type=jnp.float32)
    columns = lax.dynamic_slice_in_dim(whole, look_start, LOOK * NB, 1)
    col_tile = k + 1 + (jnp.arange(LOOK * NB) // NB).astype(jnp.int32)
    mask = row_tile[:, None] >= col_tile[None, :]
    new_columns = jnp.where(mask, columns - update, columns)
    whole = lax.dynamic_update_slice(whole, new_panel, (jnp.int32(0), start))
    whole = lax.dynamic_update_slice(whole, new_columns, (jnp.int32(0), look_start))
    return restore(whole)
```

```python
import jax
import jax.numpy as jnp
from jax import lax
from jax.experimental import pallas as pl
from jax.experimental.pallas import tpu as pltpu
from jax.sharding import PartitionSpec as P

NB = 128
LOOK = 16
VMEM_LIMIT = 48 * 1024 * 1024
F32 = jnp.float32
BF16 = jnp.bfloat16
HI = lax.Precision.HIGHEST
ANY = pl.BlockSpec(memory_space=pl.ANY)
PART = 1536
SHIFTS = (2, 1, 3)


def params():
    return pltpu.CompilerParams(vmem_limit_bytes=VMEM_LIMIT)


def z_shift(s):
    return [(z * 4 + y, (z + s) % 4 * 4 + y) for z in range(4) for y in range(4)]


def y_shift(s):
    return [(z * 4 + y, z * 4 + (y + s) % 4) for z in range(4) for y in range(4)]


def x_shift(s):
    return [(x * 2 + c, (x + s) % 4 * 2 + c) for x in range(4) for c in range(2)]


def core_swap():
    return [(i, i ^ 1) for i in range(8)]


def cast_parts(window, z, y):
    step = 512
    per = PART // step

    def body(place_ref, *refs):
        for source, target in zip(refs[:8], refs[8:]):
            target[...] = source[...].astype(BF16)

    def spec(n):
        if n < 4:
            return pl.BlockSpec((step, NB), lambda i, s: (lax.rem(s[0] + n, 4) * per + i, 0))
        return pl.BlockSpec((step, NB), lambda i, s: ((4 + lax.rem(s[1] + n, 4)) * per + i, 0))

    return pl.pallas_call(
        body,
        grid_spec=pltpu.PrefetchScalarGridSpec(
            num_scalar_prefetch=1,
            grid=(per,),
            in_specs=[spec(n) for n in range(8)],
            out_specs=[pl.BlockSpec((step, NB), lambda i, s: (i, 0))] * 8,
        ),
        out_shape=[jax.ShapeDtypeStruct((PART, NB), BF16)] * 8,
        compiler_params=params(),
        name="cast_parts",
    )(jnp.stack([z, y]), *([window] * 8))


def pick_parts(choice, first, second):
    def body(choice_ref, *refs):
        sem = refs[10]
        for half in range(2):
            for s in range(4):

                @pl.when(choice_ref[half] == s)
                def _():
                    copy = pltpu.make_async_copy(refs[4 * half + s], refs[8 + half], sem.at[half])
                    copy.start()

        for half in range(2):
            pltpu.make_async_copy(refs[4 * half], refs[8 + half], sem.at[half]).wait()

    return pl.pallas_call(
        body,
        in_specs=[pl.BlockSpec(memory_space=pltpu.SMEM)] + [ANY] * 8,
        out_specs=[ANY, ANY],
        out_shape=[jax.ShapeDtypeStruct((PART, NB), BF16)] * 2,
        scratch_shapes=[pltpu.SemaphoreType.DMA((2,))],
        compiler_params=params(),
        name="pick_parts",
    )(choice, *first, *second)


def factor(places, tile, rows):
    def body(places_ref, tile_ref, rows_ref, low_ref, inv_ref, weights_ref, work):
        t = tile_ref[...]
        row = lax.broadcasted_iota(jnp.int32, (NB, NB), 0)
        col = lax.broadcasted_iota(jnp.int32, (NB, NB), 1)
        work[:, :NB] = 0.5 * (t + t.T)
        work[:, NB:] = jnp.where(row == col, 1.0, 0.0)
        weights_ref[...] = jnp.zeros_like(weights_ref)
        sub = lax.broadcasted_iota(jnp.int32, (8, 1), 0)
        upper = []
        inverse = []
        for b in range(NB // 8):
            block = work[8 * b : 8 * b + 8, :]
            done = jnp.zeros((8, 2 * NB), F32)
            for s in range(8):
                j = 8 * b + s
                scale = lax.rsqrt(block[s : s + 1, j : j + 1])
                line = block[s : s + 1, :] * scale
                weight = jnp.where(sub > s, block[:, j : j + 1] * scale, 0.0)
                done = jnp.where(sub == s, line, done)
                block = block - weight * line
            upper.append(done[:, :NB])
            inverse.append(done[:, NB:])
            if b < NB // 8 - 1:
                work[...] -= lax.dot_general(
                    done[:, :NB], done, (((0,), (0,)), ((), ())), precision=HI, preferred_element_type=F32
                )
        up = jnp.concatenate(upper, 0)
        low_ref[...] = jnp.where(row >= col, up.T, 0.0)
        inv = jnp.where(row >= col, jnp.concatenate(inverse, 0), 0.0)
        inv_ref[...] = inv
        for n in range(2):
            half = lax.dot_general(
                inv, rows_ref[n * NB : (n + 1) * NB, :], (((1,), (1,)), ((), ())), precision=HI, preferred_element_type=F32
            )
            full = lax.dot_general(inv, half, (((0,), (0,)), ((), ())), precision=HI, preferred_element_type=F32)
            weights_ref[pl.ds(pl.multiple_of(places_ref[n] * NB, NB), NB), :] = full.astype(BF16)

    vmem = pl.BlockSpec(memory_space=pltpu.VMEM)
    return pl.pallas_call(
        body,
        in_specs=[pl.BlockSpec(memory_space=pltpu.SMEM), vmem, vmem],
        out_specs=[vmem] * 3,
        out_shape=[
            jax.ShapeDtypeStruct((NB, NB), F32),
            jax.ShapeDtypeStruct((NB, NB), F32),
            jax.ShapeDtypeStruct((LOOK * NB, NB), BF16),
        ],
        scratch_shapes=[pltpu.VMEM((NB, 2 * NB), F32)],
        compiler_params=params(),
        name="factor",
    )(places, tile, rows)


def keep_column(scalars, window, low, inv):
    step = PART

    def body(s_ref, window_ref, low_ref, inv_ref, out_ref):
        i = pl.program_id(0)
        k, p, is_panel = s_ref[0], s_ref[1], s_ref[2]

        @pl.when(is_panel == 0)
        def _():
            out_ref[...] = window_ref[...]

        @pl.when(is_panel == 1)
        def _():
            out_ref[...] = lax.dot_general(
                window_ref[...].astype(BF16),
                inv_ref[...].astype(BF16),
                (((1,), (1,)), ((), ())),
                preferred_element_type=F32,
            )

            @pl.when(i == 0)
            def _():
                for slot in range(2):
                    tile = slot * 8 + p
                    rows = pl.ds(slot * NB, NB)

                    @pl.when(tile == k)
                    def _():
                        out_ref[rows, :] = low_ref[...]

                    @pl.when(tile < k)
                    def _():
                        out_ref[rows, :] = window_ref[rows, :]

    return pl.pallas_call(
        body,
        grid_spec=pltpu.PrefetchScalarGridSpec(
            num_scalar_prefetch=1,
            grid=(window.shape[0] // step,),
            in_specs=[
                pl.BlockSpec((step, NB), lambda i, s: (i, 1 - s[3])),
                pl.BlockSpec((NB, NB), lambda i, s: (0, 0)),
                pl.BlockSpec((NB, NB), lambda i, s: (0, 0)),
            ],
            out_specs=pl.BlockSpec((step, NB), lambda i, s: (i, 1 - s[3])),
        ),
        out_shape=jax.ShapeDtypeStruct(window.shape, F32),
        compiler_params=params(),
        name="keep_column",
    )(scalars, window, low, inv)


def update(scalars, window, weights, parts, places, out):
    n = len(parts)
    s_all = jnp.concatenate([scalars, jnp.stack(places)])

    def body(s_ref, *refs):
        windows, panels, weight_ref = refs[:n], refs[n : 2 * n], refs[2 * n]
        out_hbm, buffers, sem = refs[2 * n + 2], refs[2 * n + 3], refs[2 * n + 4]
        p, j = s_ref[1], s_ref[4]
        lane = pl.multiple_of(s_ref[3] * NB, NB)
        i = pl.program_id(0)
        slot = lax.rem(i, 2)
        size = windows[0].shape[0]

        def copy_out(m, which, step):
            row = pl.multiple_of(s_ref[5 + m] * PART + step * size, size)
            return pltpu.make_async_copy(
                buffers.at[which, m], out_hbm.at[pl.ds(row, size), pl.ds(lane, NB)], sem.at[which, m]
            )

        for m in range(n):

            @pl.when(i >= 2)
            def _():
                copy_out(m, slot, i - 2).wait()

            row = s_ref[5 + m] * PART + i * size + lax.broadcasted_iota(jnp.int32, (size, NB), 0)
            tile = lax.shift_right_logical(row, 7) * 8 + p
            change = lax.dot_general(
                panels[m][...], weight_ref[...], (((1,), (0,)), ((), ())), preferred_element_type=F32
            )
            buffers[slot, m] = windows[m][...] - jnp.where(tile >= j, change, 0.0)
            copy_out(m, slot, i).start()

        @pl.when(i == pl.num_programs(0) - 1)
        def _():
            for m in range(n):
                copy_out(m, 1 - slot, i - 1).wait()
                copy_out(m, slot, i).wait()

    step = 768

    def window_spec(m):
        return pl.BlockSpec((step, NB), lambda i, s: (s[5 + m] * (PART // step) + i, s[3]))

    return pl.pallas_call(
        body,
        grid_spec=pltpu.PrefetchScalarGridSpec(
            num_scalar_prefetch=1,
            grid=(PART // step,),
            in_specs=[window_spec(m) for m in range(n)]
            + [pl.BlockSpec((step, NB), lambda i, s: (i, 0))] * n
            + [pl.BlockSpec((NB, NB), lambda i, s: (0, 0)), ANY],
            out_specs=ANY,
            scratch_shapes=[pltpu.VMEM((2, n, step, NB), F32), pltpu.SemaphoreType.DMA((2, n))],
        ),
        out_shape=jax.ShapeDtypeStruct(window.shape, F32),
        input_output_aliases={2 * n + 2: 0},
        compiler_params=params(),
        name="update",
    )(s_all, *([window] * n), *parts, weights, out)


def over_prow(block):
    pair = block + lax.ppermute(block, "prow", core_swap())
    others = [lax.ppermute(pair, "prow", x_shift(s)) for s in (2, 1, 3)]
    return pair + others[0] + others[1] + others[2]


def body(window, panel_index):
    k = panel_index[0]
    p = lax.axis_index("prow")
    q = lax.axis_index("pcol")
    z, y = q // 4, q % 4
    z0, y0 = k // 4, k % 4
    dz, dy = (z - z0) % 4, (y - y0) % 4
    slot = jnp.where(q <= k, 1, 0)
    j = slot * 16 + q
    scalars = jnp.stack([k, p, jnp.where(q == k, 1, 0), slot, j]).astype(jnp.int32)

    parts = cast_parts(window, z, y)

    got = {}
    for s in SHIFTS:
        got["z", s] = lax.ppermute(parts[s], "pcol", z_shift(s))
        got["y", s] = lax.ppermute(parts[4 + s], "pcol", y_shift(s))
    first, second = pick_parts(
        jnp.stack([dz, dy]),
        [parts[0], got["z", 1], got["z", 2], got["z", 3]],
        [parts[4], got["y", 1], got["y", 2], got["y", 3]],
    )

    tile = lax.dynamic_slice(window, (k // 8 * NB, 0), (NB, NB))
    tile = over_prow(jnp.where(p == k % 8, tile, 0.0))
    j_first = k + 1 + (p - (k + 1)) % 8
    look_rows = lax.dynamic_slice(window, (j_first // 8 * NB, 0), (2 * NB, NB))
    low, inv, weights = factor(jnp.stack([j_first % 16, (j_first + 8) % 16]), tile, look_rows)

    for s in SHIFTS:
        got["y", s] = lax.ppermute(first, "pcol", y_shift(s))
        got["z", s] = lax.ppermute(second, "pcol", z_shift(s))
    first, second = pick_parts(
        jnp.stack([dy, dz]),
        [first, got["y", 1], got["y", 2], got["y", 3]],
        [second, got["z", 1], got["z", 2], got["z", 3]],
    )

    weights = lax.all_to_all(weights, "pcol", 0, 0, tiled=True)
    weights = over_prow(lax.dynamic_slice(weights, (k * NB, 0), (NB, NB)))

    out = keep_column(scalars, window, low, inv)

    for s in SHIFTS:
        got["z", s] = lax.ppermute(first, "pcol", z_shift(s))
        got["y", s] = lax.ppermute(second, "pcol", y_shift(s))
    out = update(scalars, window, weights, [first, second], [z, 4 + y], out)
    for s in SHIFTS:
        out = update(
            scalars, window, weights, [got["z", s], got["y", s]], [(z - s) % 4, 4 + (y - s) % 4], out
        )
    return out


def solution(mesh):
    return jax.shard_map(
        body,
        mesh=mesh,
        in_specs=(P("prow", "pcol"), P()),
        out_specs=P("prow", "pcol"),
        check_vma=False,
    )
```

```python
import jax
import jax.numpy as jnp
from jax import lax
from jax.experimental import pallas as pl
from jax.experimental.pallas import tpu as pltpu
from jax.sharding import PartitionSpec as P

NB = 128
LOOK = 16
VMEM_LIMIT = 48 * 1024 * 1024
F32 = jnp.float32
BF16 = jnp.bfloat16
HI = lax.Precision.HIGHEST
ANY = pl.BlockSpec(memory_space=pl.ANY)
HBM = pl.BlockSpec(memory_space=pltpu.HBM)
SMEM = pl.BlockSpec(memory_space=pltpu.SMEM)
VMEM = pl.BlockSpec(memory_space=pltpu.VMEM)
SHARE = 16
PART = 1536
SHIFTS = (1, 3, 2)
BOTH = ("prow", "pcol")


def params():
    return pltpu.CompilerParams(vmem_limit_bytes=VMEM_LIMIT)


def z_shift(s):
    return [(z * 4 + y, (z + s) % 4 * 4 + y) for z in range(4) for y in range(4)]


def y_shift(s):
    return [(z * 4 + y, z * 4 + (y + s) % 4) for z in range(4) for y in range(4)]


def x_shift(s):
    return [(x * 2 + c, (x + s) % 4 * 2 + c) for x in range(4) for c in range(2)]


def split_shift(s, axis):
    pairs = []
    for p in range(8):
        along = z_shift(s) if (p + axis) % 2 == 0 else y_shift(s)
        pairs += [(p * 16 + a, p * 16 + b) for a, b in along]
    return pairs


def core_swap():
    return [(i, i ^ 1) for i in range(8)]


def cost(us):
    return pl.CostEstimate(flops=0, transcendentals=0, bytes_accessed=int(us * 3.5e6))


def read_half(place_ref, window_ref, buffer, sem):
    copies = []
    for n in range(4):
        part = place_ref[0] * 4 + lax.rem(place_ref[1] + n, 4)
        rows = pl.ds(pl.multiple_of(part * PART, PART), PART)
        copies.append(pltpu.make_async_copy(window_ref.at[rows, pl.ds(0, NB)], buffer.at[n], sem.at[n]))
    return copies


def cast_half(window, half, first):
    def body(place_ref, window_ref, out_ref, buffer, sem):
        copies = read_half(place_ref, window_ref, buffer, sem)
        for copy in copies:
            copy.start()
        for n in range(4):
            copies[n].wait()
            out_ref[n * PART : (n + 1) * PART, :] = buffer[n].astype(BF16)

    return pl.pallas_call(
        body,
        in_specs=[SMEM, HBM],
        out_specs=VMEM,
        out_shape=jax.ShapeDtypeStruct((4 * PART, NB), BF16),
        scratch_shapes=[pltpu.VMEM((4, PART, NB), F32), pltpu.SemaphoreType.DMA((4,))],
        compiler_params=params(),
        cost_estimate=cost(2.0),
        name="cast_half",
    )(jnp.stack([half, first]).astype(jnp.int32), window)


def pair_up(window, half, first, partners):
    def body(place_ref, window_ref, partners_ref, *refs):
        outs, buffer, sem = refs[:4], refs[4], refs[5]
        copies = read_half(place_ref, window_ref, buffer, sem)
        for copy in copies:
            copy.start()
        for n in range(4):
            outs[n][PART:, :] = partners_ref[n * PART : (n + 1) * PART, :]
        for n in range(4):
            copies[n].wait()
            outs[n][:PART, :] = buffer[n].astype(BF16)

    return pl.pallas_call(
        body,
        in_specs=[SMEM, HBM, VMEM],
        out_specs=[VMEM] * 4,
        out_shape=[jax.ShapeDtypeStruct((2 * PART, NB), BF16)] * 4,
        scratch_shapes=[pltpu.VMEM((4, PART, NB), F32), pltpu.SemaphoreType.DMA((4,))],
        compiler_params=params(),
        cost_estimate=cost(2.5),
        name="pair_up",
    )(jnp.stack([half, first]).astype(jnp.int32), window, partners)


def cut_shares(places, tiles):
    def body(places_ref, *refs):
        out_ref, stack = refs[4], refs[5]
        for n in range(4):
            stack[n * 6 * NB : (n + 1) * 6 * NB, :] = refs[n][...]

        def share(n):
            row = places_ref[n] * NB + places_ref[LOOK + 1] * SHARE
            return stack[pl.ds(pl.multiple_of(row, SHARE), SHARE), :]

        for n in range(LOOK):
            out_ref[2 * n * SHARE : (2 * n + 1) * SHARE, :] = share(0)
            out_ref[(2 * n + 1) * SHARE : (2 * n + 2) * SHARE, :] = share(n + 1)

    return pl.pallas_call(
        body,
        in_specs=[SMEM] + [VMEM] * 4,
        out_specs=VMEM,
        out_shape=jax.ShapeDtypeStruct((2 * LOOK * SHARE, NB), BF16),
        scratch_shapes=[pltpu.VMEM((24 * NB, NB), BF16)],
        compiler_params=params(),
        cost_estimate=cost(1.0),
        name="cut_shares",
    )(places, *tiles)


def pick(choice, arrays):
    return jnp.where(
        choice < 2, jnp.where(choice == 0, arrays[0], arrays[1]), jnp.where(choice == 2, arrays[2], arrays[3])
    )


def factor(places, shares):
    block_rows = 16

    def body(places_ref, *refs):
        low_ref, inv_ref, weights_ref, work, stack = refs[4:]
        for n in range(4):
            stack[n * 4 * SHARE : (n + 1) * 4 * SHARE, :] = refs[n][...]

        def tile_at(n):
            shares = []
            for p in range(8):
                row = lax.rem(places_ref[0] - p // 2 + 4, 4) * 4 * SHARE + (p % 2 * 2 + n) * SHARE
                shares.append(stack[pl.ds(pl.multiple_of(row, SHARE), SHARE), :])
            return jnp.concatenate(shares, 0)

        t = tile_at(0).astype(F32)
        row = lax.broadcasted_iota(jnp.int32, (NB, NB), 0)
        col = lax.broadcasted_iota(jnp.int32, (NB, NB), 1)
        work[:, :NB] = 0.5 * (t + t.T)
        work[:, NB:] = jnp.where(row == col, 1.0, 0.0)
        sub = lax.broadcasted_iota(jnp.int32, (block_rows, NB), 0)
        upper = []
        inverse = []
        for b in range(NB // block_rows):
            base = block_rows * b
            left = work[base : base + block_rows, :NB]
            right = work[base : base + block_rows, NB:]
            columns = [
                jnp.broadcast_to(left[:, base + s : base + s + 1], (block_rows, NB)) for s in range(block_rows)
            ]
            done_left = left
            done_right = right
            for s in range(block_rows):
                scale = lax.rsqrt(columns[s][s : s + 1, :])
                weight = columns[s] * scale
                for r in range(s + 1, block_rows):
                    columns[r] = columns[r] - weight * weight[r : r + 1, :]
                below = jnp.where(sub > s, weight, 0.0)
                line_left = left[s : s + 1, :] * scale
                line_right = right[s : s + 1, :] * scale
                done_left = jnp.where(sub == s, line_left, done_left)
                done_right = jnp.where(sub == s, line_right, done_right)
                left = left - below * line_left
                right = right - below * line_right
            upper.append(done_left)
            inverse.append(done_right)
            if base + block_rows < NB:
                work[...] -= lax.dot_general(
                    done_left,
                    jnp.concatenate([done_left, done_right], 1),
                    (((0,), (0,)), ((), ())),
                    precision=HI,
                    preferred_element_type=F32,
                )
        up = jnp.concatenate(upper, 0)
        low_ref[...] = jnp.where(row >= col, up.T, 0.0)
        inv = jnp.where(row >= col, jnp.concatenate(inverse, 0), 0.0)
        inv_ref[...] = inv
        tile = tile_at(1).astype(F32)
        half = lax.dot_general(inv, tile, (((1,), (1,)), ((), ())), precision=HI, preferred_element_type=F32)
        full = lax.dot_general(inv, half, (((0,), (0,)), ((), ())), precision=HI, preferred_element_type=F32)
        weights_ref[...] = full.astype(BF16)

    return pl.pallas_call(
        body,
        in_specs=[SMEM] + [VMEM] * 4,
        out_specs=[VMEM] * 3,
        out_shape=[
            jax.ShapeDtypeStruct((NB, NB), F32),
            jax.ShapeDtypeStruct((NB, NB), F32),
            jax.ShapeDtypeStruct((NB, NB), BF16),
        ],
        scratch_shapes=[pltpu.VMEM((NB, 2 * NB), F32), pltpu.VMEM((16 * SHARE, NB), BF16)],
        compiler_params=params(),
        cost_estimate=cost(10.0),
        name="factor",
    )(places, *shares)


def column_copies(source, buffer, target, lane, sem, count):
    size = buffer.shape[0] // count
    lanes = pl.ds(pl.multiple_of(lane * NB, NB), NB)
    into, out = [], []
    for n in range(count):
        rows = pl.ds(n * size, size)
        into.append(pltpu.make_async_copy(source.at[rows, lanes], buffer.at[rows], sem.at[0, n]))
        out.append(pltpu.make_async_copy(buffer.at[rows], target.at[rows, lanes], sem.at[1, n]))
    return into, out


def keep_column(scalars, window):
    def body(s_ref, window_ref, out_ref, buffer, sem):
        @pl.when(s_ref[2] == 0)
        def _():
            into, out = column_copies(window_ref, buffer, out_ref, 1 - s_ref[3], sem, 4)
            for copy in into:
                copy.start()
            for first, second in zip(into, out):
                first.wait()
                second.start()
            for copy in out:
                copy.wait()

    return pl.pallas_call(
        body,
        in_specs=[SMEM, HBM],
        out_specs=HBM,
        out_shape=jax.ShapeDtypeStruct(window.shape, F32),
        scratch_shapes=[pltpu.VMEM((window.shape[0], NB), F32), pltpu.SemaphoreType.DMA((2, 4))],
        compiler_params=params(),
        cost_estimate=cost(5.5),
        name="keep_column",
    )(scalars, window)


def write_panel(scalars, window, low, inv, out):
    count = 4
    size = window.shape[0] // count

    def body(s_ref, window_ref, low_ref, inv_ref, _, out_ref, buffer, sem):
        k, p = s_ref[0], s_ref[1]

        @pl.when(s_ref[2] == 1)
        def _():
            into, out = column_copies(window_ref, buffer, out_ref, 0, sem, count)
            for copy in into:
                copy.start()
            high = inv_ref[...].astype(BF16)
            for n in range(count):
                into[n].wait()
                if n == 0:
                    head = buffer[0 : 2 * NB, :]
                for t in range(size // 256):
                    rows = slice(n * size + t * 256, n * size + (t + 1) * 256)
                    buffer[rows, :] = lax.dot_general(
                        buffer[rows, :].astype(BF16), high, (((1,), (1,)), ((), ())), preferred_element_type=F32
                    )
                if n == 0:
                    for slot in range(2):
                        tile = slot * 8 + p
                        rows = pl.ds(slot * NB, NB)

                        @pl.when(tile == k)
                        def _():
                            buffer[rows, :] = low_ref[...]

                        @pl.when(tile < k)
                        def _():
                            buffer[rows, :] = head[slot * NB : (slot + 1) * NB, :]

                out[n].start()
            for copy in out:
                copy.wait()

    return pl.pallas_call(
        body,
        in_specs=[SMEM, HBM, VMEM, VMEM, HBM],
        out_specs=HBM,
        out_shape=jax.ShapeDtypeStruct(window.shape, F32),
        scratch_shapes=[pltpu.VMEM((window.shape[0], NB), F32), pltpu.SemaphoreType.DMA((2, count))],
        input_output_aliases={4: 0},
        compiler_params=params(),
        cost_estimate=cost(1.0),
        name="write_panel",
    )(scalars, window, low, inv, out)


def hold(scalars, window, places):
    n = len(places)

    def body(s_ref, window_ref, out_ref, sem):
        lanes = pl.ds(pl.multiple_of(s_ref[3] * NB, NB), NB)
        copies = [
            pltpu.make_async_copy(
                window_ref.at[pl.ds(pl.multiple_of(s_ref[5 + m] * PART, PART), PART), lanes], out_ref.at[m], sem.at[m]
            )
            for m in range(n)
        ]
        for copy in copies:
            copy.start()
        for copy in copies:
            copy.wait()

    return pl.pallas_call(
        body,
        in_specs=[SMEM, HBM],
        out_specs=VMEM,
        out_shape=jax.ShapeDtypeStruct((n, PART, NB), F32),
        scratch_shapes=[pltpu.SemaphoreType.DMA((n,))],
        compiler_params=params(),
        cost_estimate=cost(1.5),
        name="hold",
    )(jnp.concatenate([scalars, jnp.stack(places).astype(jnp.int32)]), window)


def update(scalars, window, weights, parts, places, out, held=None):
    n = len(parts)
    size = PART // 2
    blocks = [(m, i) for m in range(n) for i in range(2)]
    s_all = jnp.concatenate([scalars, jnp.stack(places).astype(jnp.int32)])
    source = window if held is None else held[0]

    def body(s_ref, source_ref, weight_ref, *refs):
        panels, out_ref = refs[:n], refs[n + 1]
        buffer, sem = refs[n + 2 :]
        p, j = s_ref[1], s_ref[4]
        lanes = pl.ds(pl.multiple_of(s_ref[3] * NB, NB), NB)

        def rows(m, i):
            return pl.ds(pl.multiple_of(s_ref[5 + m] * PART + i * size, size), size)

        def read(m, i):
            return pltpu.make_async_copy(source_ref.at[rows(m, i), lanes], buffer.at[m, i], sem.at[0, m, i])

        def write(m, i):
            return pltpu.make_async_copy(buffer.at[m, i], out_ref.at[rows(m, i), lanes], sem.at[1, m, i])

        if held is None:
            for m, i in blocks:
                read(m, i).start()
        for m, i in blocks:
            first = parts[m][1] * PART + i * size
            if held is None:
                read(m, i).wait()
            for t in range(size // 256):
                change = lax.dot_general(
                    panels[m][first + t * 256 : first + (t + 1) * 256, :],
                    weight_ref[...],
                    (((1,), (0,)), ((), ())),
                    preferred_element_type=F32,
                )
                for u in range(2):
                    at = t * 256 + u * NB
                    tile = (s_ref[5 + m] * (PART // NB) + (i * size + at) // NB) * 8 + p
                    if held is None:
                        old = buffer[m, i, at : at + NB, :]
                    else:
                        old = source_ref[held[1] + m, i * size + at : i * size + at + NB, :]
                    buffer[m, i, at : at + NB, :] = old - jnp.where(tile >= j, change[u * NB : (u + 1) * NB, :], 0.0)
            write(m, i).start()
        for m, i in blocks:
            write(m, i).wait()

    return pl.pallas_call(
        body,
        in_specs=[SMEM, HBM if held is None else VMEM, VMEM] + [VMEM] * n + [HBM],
        out_specs=HBM,
        out_shape=jax.ShapeDtypeStruct(window.shape, F32),
        scratch_shapes=[
            pltpu.VMEM((n, 2, size, NB), F32),
            pltpu.SemaphoreType.DMA((2, n, 2)),
        ],
        input_output_aliases={3 + n: 0},
        compiler_params=params(),
        cost_estimate=cost(1.0 + 0.8 * n),
        name="update",
    )(s_all, source, weights, *[part[0] for part in parts], out)


def turn(s):
    return [(n * 2 + c, (n + (s if c == 0 else -s)) % 4 * 2 + c) for n in range(4) for c in range(2)]


def pair_of(block, c):
    partner = lax.ppermute(block, "prow", core_swap())
    return jnp.where(c == 0, jnp.concatenate([block, partner]), jnp.concatenate([partner, block]))


def over_rows(block, pair, c):
    n = block.shape[0]
    beside = lax.ppermute(pair, "prow", turn(1))
    across = lax.ppermute(block, "prow", x_shift(2))
    got = jnp.concatenate([beside, across])
    other = lax.ppermute(got, "prow", core_swap())
    far = jnp.where(
        c == 0, jnp.concatenate([across, other[2 * n :]]), jnp.concatenate([other[2 * n :], across])
    )
    one = jnp.where(c == 0, beside, other[: 2 * n])
    three = jnp.where(c == 0, other[: 2 * n], beside)
    return [pair, one, far, three]


def body(window, panel_index):
    k = panel_index[0]
    p = lax.axis_index("prow")
    q = lax.axis_index("pcol")
    z, y = q // 4, q % 4
    x, c = p // 2, p % 2
    z0, y0 = k // 4, k % 4
    dz, dy = (z - z0) % 4, (y - y0) % 4
    slot = jnp.where(q <= k, 1, 0)
    j = slot * 16 + q
    scalars = jnp.stack([k, p, jnp.where(q == k, 1, 0), slot, j]).astype(jnp.int32)

    along, across = jnp.where(c == 0, z, y), jnp.where(c == 0, y, z)
    d_along, d_across = jnp.where(c == 0, dz, dy), jnp.where(c == 0, dy, dz)
    others = lax.ppermute(cast_half(window, 1 - c, across), "prow", core_swap())
    own = lax.dynamic_slice(window, (k // 8 * NB, 0), (3 * NB, NB)).astype(BF16)
    pair = pair_of(own, c)
    pair, others = lax.optimization_barrier((pair, others))
    messages = pair_up(window, c, along, others)
    messages, own, pair = lax.optimization_barrier((messages, own, pair))

    moved = [messages[0]] + [lax.ppermute(messages[s], BOTH, split_shift(s, 0)) for s in (1, 2, 3)]

    tiles = over_rows(own, pair, c)
    column = jnp.arange(LOOK)
    look = jnp.concatenate([jnp.reshape(k, (1,)), column + jnp.where(column <= k, 16, 0)])
    at = (x - look % 8 // 2) % 4 * 6 + look % 2 * 3 + look // 8 - k // 8
    shares = cut_shares(jnp.concatenate([at, jnp.reshape(p, (1,))]).astype(jnp.int32), tiles)
    shares = lax.all_to_all(shares, "pcol", 0, 0, tiled=True)
    moved, shares = lax.optimization_barrier((moved, shares))
    message = pick(d_along, moved)

    moved = [message] + [lax.ppermute(message, BOTH, split_shift(s, 1)) for s in (1, 2, 3)]
    share = lax.dynamic_slice(shares, (k * 2 * SHARE, 0), (2 * SHARE, NB))
    low, inv, weights = factor(jnp.reshape(x, (1,)).astype(jnp.int32), over_rows(share, pair_of(share, c), c))
    out = keep_column(scalars, window)
    out = write_panel(scalars, window, low, inv, out)
    moved, out, weights = lax.optimization_barrier((moved, out, weights))
    message = pick(d_across, moved)

    gathered = [message] + [lax.ppermute(message, BOTH, split_shift(s, 0)) for s in (1, 2, 3)]

    def places_of(s):
        return [4 * c + (along - s) % 4, 4 * (1 - c) + (across - s) % 4]

    def swapped(block):
        return lax.ppermute(block, "prow", core_swap())

    out = update(scalars, window, weights, [(gathered[0], 0), (swapped(gathered[0]), 1)], places_of(0), out)
    gathered, out = lax.optimization_barrier((gathered, out))
    others = [swapped(gathered[s]) for s in SHIFTS]
    out = update(
        scalars, window, weights, [(gathered[s], 0) for s in SHIFTS], [places_of(s)[0] for s in SHIFTS], out
    )
    others, out = lax.optimization_barrier((others, out))
    return update(
        scalars, window, weights, [(other, 1) for other in others], [places_of(s)[1] for s in SHIFTS], out
    )


def solution(mesh):
    return jax.shard_map(
        body,
        mesh=mesh,
        in_specs=(P("prow", "pcol"), P()),
        out_specs=P("prow", "pcol"),
        check_vma=False,
    )
```

```python
import jax
import jax.numpy as jnp
from jax import lax
from jax.experimental import pallas as pl
from jax.experimental.pallas import tpu as pltpu
from jax.sharding import PartitionSpec as P

NB = 128
LOOK = 16
ORDER = ((1, 3, 2), (2, 3, 1), (2, 3, 1), (2, 3, 1))
VMEM_LIMIT = 44 * 1024 * 1024
F32 = jnp.float32
BF16 = jnp.bfloat16
HI = lax.Precision.HIGHEST
ANY = pl.BlockSpec(memory_space=pl.ANY)
HBM = pl.BlockSpec(memory_space=pltpu.HBM)
SMEM = pl.BlockSpec(memory_space=pltpu.SMEM)
VMEM = pl.BlockSpec(memory_space=pltpu.VMEM)
SHARE = 64
PART = 1536
BOTH = ("prow", "pcol")


def params():
    return pltpu.CompilerParams(vmem_limit_bytes=VMEM_LIMIT)


def z_shift(s):
    return [(z * 4 + y, (z + s) % 4 * 4 + y) for z in range(4) for y in range(4)]


def y_shift(s):
    return [(z * 4 + y, z * 4 + (y + s) % 4) for z in range(4) for y in range(4)]


def x_shift(s):
    return [(x * 2 + c, (x + s) % 4 * 2 + c) for x in range(4) for c in range(2)]


def split_shift(s, axis):
    pairs = []
    for p in range(8):
        along = z_shift(s) if (p + axis) % 2 == 0 else y_shift(s)
        pairs += [(p * 16 + a, p * 16 + b) for a, b in along]
    return pairs


def core_swap():
    return [(i, i ^ 1) for i in range(8)]


def cost(us):
    return pl.CostEstimate(flops=0, transcendentals=0, bytes_accessed=int(us * 3.5e6))


def read_half(place_ref, window_ref, buffer, sem):
    copies = []
    for n in range(4):
        part = place_ref[0] * 4 + lax.rem(place_ref[1] + n, 4)
        rows = pl.ds(pl.multiple_of(part * PART, PART), PART)
        copies.append(pltpu.make_async_copy(window_ref.at[rows, pl.ds(0, NB)], buffer.at[n], sem.at[n]))
    return copies


def cast_half(window, half, first):
    def body(place_ref, window_ref, out_ref, buffer, sem):
        copies = read_half(place_ref, window_ref, buffer, sem)
        for copy in copies:
            copy.start()
        for n in range(4):
            copies[n].wait()
            out_ref[n * PART : (n + 1) * PART, :] = buffer[n].astype(BF16)

    return pl.pallas_call(
        body,
        in_specs=[SMEM, HBM],
        out_specs=VMEM,
        out_shape=jax.ShapeDtypeStruct((4 * PART, NB), BF16),
        scratch_shapes=[pltpu.VMEM((4, PART, NB), F32), pltpu.SemaphoreType.DMA((4,))],
        compiler_params=params(),
        cost_estimate=cost(2.0),
        name="cast_half",
    )(jnp.stack([half, first]).astype(jnp.int32), window)


def pair_up(window, half, first, partners):
    def body(place_ref, window_ref, partners_ref, *refs):
        outs, buffer, paired, sem = refs[:4], refs[4], refs[5], refs[6]
        copies = read_half(place_ref, window_ref, buffer, sem)
        for copy in copies:
            copy.start()
        writes = [pltpu.make_async_copy(paired.at[n], outs[n], sem.at[4 + n]) for n in range(4)]
        for n in (1, 3, 2, 0):
            paired[n, PART:, :] = partners_ref[n * PART : (n + 1) * PART, :]
        for n in range(4):
            copies[n].wait()
            paired[n, :PART, :] = buffer[n].astype(BF16)
            writes[n].start()
        for write in writes:
            write.wait()

    return pl.pallas_call(
        body,
        in_specs=[SMEM, HBM, VMEM],
        out_specs=[ANY] * 4,
        out_shape=[jax.ShapeDtypeStruct((2 * PART, NB), BF16)] * 4,
        scratch_shapes=[
            pltpu.VMEM((4, PART, NB), F32),
            pltpu.VMEM((4, 2 * PART, NB), BF16),
            pltpu.SemaphoreType.DMA((8,)),
        ],
        compiler_params=params(),
        cost_estimate=cost(2.5),
        name="pair_up",
    )(jnp.stack([half, first]).astype(jnp.int32), window, partners)


def pick(choice, arrays, order):
    choice = jnp.where(choice == 0, 0, sum(jnp.where(choice == s, n + 1, 0) for n, s in enumerate(order)))
    return jnp.where(
        choice < 2, jnp.where(choice == 0, arrays[0], arrays[1]), jnp.where(choice == 2, arrays[2], arrays[3])
    )


def factor(places, tiles):
    block_rows = 16

    def body(places_ref, *refs):
        low_ref, inv_ref, weights_ref, work, stack, rows = refs[4:]
        for n in range(4):
            stack[n * 6 * NB : (n + 1) * 6 * NB, :] = refs[n][...]

        def tile_at(n):
            return stack[pl.ds(pl.multiple_of(places_ref[n] * NB, NB), NB), :]

        t = tile_at(0).astype(F32)
        row = lax.broadcasted_iota(jnp.int32, (NB, NB), 0)
        col = lax.broadcasted_iota(jnp.int32, (NB, NB), 1)
        work[:, :NB] = 0.5 * (t + t.T)
        work[:, NB:] = jnp.where(row == col, 1.0, 0.0)
        sub = lax.broadcasted_iota(jnp.int32, (block_rows, NB), 0)
        upper = []
        inverse = []
        for b in range(NB // block_rows):
            base = block_rows * b
            left = work[base : base + block_rows, :NB]
            right = work[base : base + block_rows, NB:]
            columns = [
                jnp.broadcast_to(left[:, base + s : base + s + 1], (block_rows, NB)) for s in range(block_rows)
            ]
            done_left = left
            done_right = right
            for s in range(block_rows):
                scale = lax.rsqrt(columns[s][s : s + 1, :])
                weight = columns[s] * scale
                for r in range(s + 1, block_rows):
                    columns[r] = columns[r] - weight * weight[r : r + 1, :]
                below = jnp.where(sub > s, weight, 0.0)
                line_left = left[s : s + 1, :] * scale
                line_right = right[s : s + 1, :] * scale
                done_left = jnp.where(sub == s, line_left, done_left)
                done_right = jnp.where(sub == s, line_right, done_right)
                left = left - below * line_left
                right = right - below * line_right
            upper.append(done_left)
            inverse.append(done_right)
            if base + block_rows < NB:
                work[...] -= lax.dot_general(
                    done_left,
                    jnp.concatenate([done_left, done_right], 1),
                    (((0,), (0,)), ((), ())),
                    precision=HI,
                    preferred_element_type=F32,
                )
        up = jnp.concatenate(upper, 0)
        low_ref[...] = jnp.where(row >= col, up.T, 0.0)
        inv = jnp.where(row >= col, jnp.concatenate(inverse, 0), 0.0)
        inv_ref[...] = inv
        both = lax.dot_general(inv, inv, (((0,), (0,)), ((), ())), precision=HI, preferred_element_type=F32)
        high = both.astype(BF16)
        rest = (both - high.astype(F32)).astype(BF16)
        for n in range(1, LOOK + 1):
            row = places_ref[n] * NB + places_ref[2 * LOOK + 1] * SHARE
            place = pl.multiple_of(places_ref[LOOK + n] * SHARE, SHARE)
            rows[pl.ds(place, SHARE), :] = stack[pl.ds(pl.multiple_of(row, SHARE), SHARE), :]
        full = lax.dot_general(rows[...], high, (((1,), (0,)), ((), ())), preferred_element_type=F32)
        full += lax.dot_general(rows[...], rest, (((1,), (0,)), ((), ())), preferred_element_type=F32)
        weights_ref[...] = full.astype(BF16)

    return pl.pallas_call(
        body,
        in_specs=[SMEM] + [VMEM] * 4,
        out_specs=[VMEM] * 3,
        out_shape=[
            jax.ShapeDtypeStruct((NB, NB), F32),
            jax.ShapeDtypeStruct((NB, NB), F32),
            jax.ShapeDtypeStruct((LOOK * SHARE, NB), BF16),
        ],
        scratch_shapes=[pltpu.VMEM((NB, 2 * NB), F32), pltpu.VMEM((24 * NB, NB), BF16), pltpu.VMEM((LOOK * SHARE, NB), BF16)],
        compiler_params=params(),
        cost_estimate=cost(10.0),
        name="factor",
    )(places, *tiles)


def column_copies(source, buffer, target, lane, sem, count):
    size = buffer.shape[0] // count
    lanes = pl.ds(pl.multiple_of(lane * NB, NB), NB)
    into, out = [], []
    for n in range(count):
        rows = pl.ds(n * size, size)
        into.append(pltpu.make_async_copy(source.at[rows, lanes], buffer.at[rows], sem.at[0, n]))
        out.append(pltpu.make_async_copy(buffer.at[rows], target.at[rows, lanes], sem.at[1, n]))
    return into, out


def keep_column(scalars, window):
    def body(s_ref, window_ref, out_ref, buffer, sem):
        @pl.when(s_ref[2] == 0)
        def _():
            into, out = column_copies(window_ref, buffer, out_ref, 1 - s_ref[3], sem, 4)
            for copy in into:
                copy.start()
            for first, second in zip(into, out):
                first.wait()
                second.start()
            for copy in out:
                copy.wait()

    return pl.pallas_call(
        body,
        in_specs=[SMEM, HBM],
        out_specs=HBM,
        out_shape=jax.ShapeDtypeStruct(window.shape, F32),
        scratch_shapes=[pltpu.VMEM((window.shape[0], NB), F32), pltpu.SemaphoreType.DMA((2, 4))],
        compiler_params=params(),
        cost_estimate=cost(5.5),
        name="keep_column",
    )(scalars, window)


def write_panel(scalars, window, low, inv, out):
    count = 4
    size = window.shape[0] // count

    def body(s_ref, window_ref, low_ref, inv_ref, _, out_ref, buffer, sem):
        k, p = s_ref[0], s_ref[1]

        @pl.when(s_ref[2] == 1)
        def _():
            into, out = column_copies(window_ref, buffer, out_ref, 0, sem, count)
            for copy in into:
                copy.start()
            high = inv_ref[...].astype(BF16)
            for n in range(count):
                into[n].wait()
                if n == 0:
                    head = buffer[0 : 2 * NB, :]
                for t in range(size // 256):
                    rows = slice(n * size + t * 256, n * size + (t + 1) * 256)
                    buffer[rows, :] = lax.dot_general(
                        buffer[rows, :].astype(BF16), high, (((1,), (1,)), ((), ())), preferred_element_type=F32
                    )
                if n == 0:
                    for slot in range(2):
                        tile = slot * 8 + p
                        rows = pl.ds(slot * NB, NB)

                        @pl.when(tile == k)
                        def _():
                            buffer[rows, :] = low_ref[...]

                        @pl.when(tile < k)
                        def _():
                            buffer[rows, :] = head[slot * NB : (slot + 1) * NB, :]

                out[n].start()
            for copy in out:
                copy.wait()

    return pl.pallas_call(
        body,
        in_specs=[SMEM, HBM, VMEM, VMEM, HBM],
        out_specs=HBM,
        out_shape=jax.ShapeDtypeStruct(window.shape, F32),
        scratch_shapes=[pltpu.VMEM((window.shape[0], NB), F32), pltpu.SemaphoreType.DMA((2, count))],
        input_output_aliases={4: 0},
        compiler_params=params(),
        cost_estimate=cost(1.0),
        name="write_panel",
    )(scalars, window, low, inv, out)


def update(scalars, window, weights, parts, places, out):
    n = len(parts)
    size = PART // 2
    blocks = [(m, i) for m in range(n) for i in range(2)]
    s_all = jnp.concatenate([scalars, jnp.stack(places).astype(jnp.int32)])

    def body(s_ref, window_ref, weight_ref, *refs):
        panels, out_ref = refs[:n], refs[n + 1]
        buffer, sem = refs[n + 2 :]
        p, j = s_ref[1], s_ref[4]
        lanes = pl.ds(pl.multiple_of(s_ref[3] * NB, NB), NB)

        def rows(m, i):
            return pl.ds(pl.multiple_of(s_ref[5 + m] * PART + i * size, size), size)

        def read(m, i):
            return pltpu.make_async_copy(window_ref.at[rows(m, i), lanes], buffer.at[m, i], sem.at[0, m, i])

        def write(m, i):
            return pltpu.make_async_copy(buffer.at[m, i], out_ref.at[rows(m, i), lanes], sem.at[1, m, i])

        for m, i in blocks:
            read(m, i).start()
        for m, i in blocks:
            read(m, i).wait()
            for t in range(size // 256):
                change = lax.dot_general(
                    panels[m][i * size + t * 256 : i * size + (t + 1) * 256, :],
                    weight_ref[...],
                    (((1,), (1,)), ((), ())),
                    preferred_element_type=F32,
                )
                for u in range(2):
                    at = t * 256 + u * NB
                    tile = (s_ref[5 + m] * (PART // NB) + (i * size + at) // NB) * 8 + p
                    old = buffer[m, i, at : at + NB, :]
                    buffer[m, i, at : at + NB, :] = old - jnp.where(tile >= j, change[u * NB : (u + 1) * NB, :], 0.0)
            write(m, i).start()
        for m, i in blocks:
            write(m, i).wait()

    return pl.pallas_call(
        body,
        in_specs=[SMEM, HBM, VMEM] + [VMEM] * n + [HBM],
        out_specs=HBM,
        out_shape=jax.ShapeDtypeStruct(window.shape, F32),
        scratch_shapes=[
            pltpu.VMEM((n, 2, size, NB), F32),
            pltpu.SemaphoreType.DMA((2, n, 2)),
        ],
        input_output_aliases={3 + n: 0},
        compiler_params=params(),
        cost_estimate=cost(1.0 + 0.8 * n),
        name="update",
    )(s_all, window, weights, *parts, out)


def turn(s):
    return [(n * 2 + c, (n + (s if c == 0 else -s)) % 4 * 2 + c) for n in range(4) for c in range(2)]


def stage(arrays, axis, order):
    return [arrays[0]] + [lax.ppermute(arrays[s], BOTH, split_shift(s, axis)) for s in order]


def side_by_side(block, partner, c):
    return jnp.where(c == 0, jnp.concatenate([block, partner]), jnp.concatenate([partner, block]))


def send_rows(block, pair):
    return jnp.concatenate([lax.ppermute(pair, "prow", turn(1)), lax.ppermute(block, "prow", x_shift(2))])


def over_rows(pair, got, c):
    n = pair.shape[0] // 2
    other = lax.ppermute(got, "prow", core_swap())
    beside, across = got[: 2 * n], got[2 * n :]
    far = jnp.where(c == 0, jnp.concatenate([across, other[2 * n :]]), jnp.concatenate([other[2 * n :], across]))
    one = jnp.where(c == 0, beside, other[: 2 * n])
    three = jnp.where(c == 0, other[: 2 * n], beside)
    return [pair, one, far, three]


def body(window, panel_index):
    k = panel_index[0]
    p = lax.axis_index("prow")
    q = lax.axis_index("pcol")
    z, y = q // 4, q % 4
    x, c = p // 2, p % 2
    z0, y0 = k // 4, k % 4
    dz, dy = (z - z0) % 4, (y - y0) % 4
    slot = jnp.where(q <= k, 1, 0)
    j = slot * 16 + q
    scalars = jnp.stack([k, p, jnp.where(q == k, 1, 0), slot, j]).astype(jnp.int32)

    along, across = jnp.where(c == 0, z, y), jnp.where(c == 0, y, z)
    d_along, d_across = jnp.where(c == 0, dz, dy), jnp.where(c == 0, dy, dz)
    others = lax.ppermute(cast_half(window, 1 - c, across), "prow", core_swap())
    own = lax.dynamic_slice(window, (k // 8 * NB, 0), (3 * NB, NB)).astype(BF16)
    partner = lax.ppermute(own, "prow", core_swap())
    partner, others = lax.optimization_barrier((partner, others))
    messages = pair_up(window, c, along, others)
    messages, own, partner, keep_scalars = lax.optimization_barrier((messages, own, partner, scalars))

    moved = stage(messages, 0, ORDER[0])
    pair = side_by_side(own, partner, c)
    got = send_rows(own, pair)
    out = keep_column(keep_scalars, window)
    moved, got, out = lax.optimization_barrier((moved, got, out))
    message = pick(d_along, moved, ORDER[0])

    message, got = lax.optimization_barrier((message, got))
    moved = stage([message] * 4, 1, ORDER[1])

    tiles = over_rows(pair, got, c)
    look = k + jnp.arange(LOOK + 1)
    at = (x - look % 8 // 2) % 4 * 6 + look % 2 * 3 + look // 8 - k // 8
    places = jnp.concatenate([at, look[1:] % 16, jnp.reshape(c, (1,))])
    low, inv, weights = factor(places.astype(jnp.int32), tiles)
    weights = lax.all_to_all(weights, "pcol", 0, 0, tiled=True)
    moved, weights = lax.optimization_barrier((moved, weights))
    message = pick(d_across, moved, ORDER[1])

    message, weights, low = lax.optimization_barrier((message, weights, low))
    mine = message[:PART]
    other = lax.ppermute(message[PART:], "prow", core_swap())
    first = stage([mine] * 4, 0, ORDER[2])
    second = stage([other] * 4, 1, ORDER[3])
    places = [4 * c + (along - s) % 4 for s in (0,) + ORDER[2]] + [4 * (1 - c) + (across - s) % 4 for s in (0,) + ORDER[3]]

    weights = lax.dynamic_slice(weights, (k * SHARE, 0), (SHARE, NB))
    weights = side_by_side(weights, lax.ppermute(weights, "prow", core_swap()), c)
    out = write_panel(scalars, window, low, inv, out)
    out = update(scalars, window, weights, [mine, other], places[::4], out)
    first, second, out = lax.optimization_barrier((first, second, out))
    return update(scalars, window, weights, first[1:] + second[1:], places[1:4] + places[5:], out)


def solution(mesh):
    return jax.shard_map(
        body,
        mesh=mesh,
        in_specs=(P("prow", "pcol"), P()),
        out_specs=P("prow", "pcol"),
        check_vma=False,
    )
```

```python
import jax
import jax.numpy as jnp
from jax import lax
from jax.experimental import pallas as pl
from jax.experimental.pallas import tpu as pltpu
from jax.sharding import PartitionSpec as P

NB = 128
LOOK = 16
ORDER = ((1, 3, 2), (2, 3, 1), (2, 3, 1), (2, 3, 1))
VMEM_LIMIT = 42 * 1024 * 1024
F32 = jnp.float32
BF16 = jnp.bfloat16
HI = lax.Precision.HIGHEST
ANY = pl.BlockSpec(memory_space=pl.ANY)
HBM = pl.BlockSpec(memory_space=pltpu.HBM)
SMEM = pl.BlockSpec(memory_space=pltpu.SMEM)
VMEM = pl.BlockSpec(memory_space=pltpu.VMEM)
SHARE = 64
PART = 1536
BOTH = ("prow", "pcol")


def params():
    return pltpu.CompilerParams(vmem_limit_bytes=VMEM_LIMIT)


def z_shift(s):
    return [(z * 4 + y, (z + s) % 4 * 4 + y) for z in range(4) for y in range(4)]


def y_shift(s):
    return [(z * 4 + y, z * 4 + (y + s) % 4) for z in range(4) for y in range(4)]


def x_shift(s):
    return [(x * 2 + c, (x + s) % 4 * 2 + c) for x in range(4) for c in range(2)]


def split_shift(s, axis):
    pairs = []
    for p in range(8):
        along = z_shift(s) if (p + axis) % 2 == 0 else y_shift(s)
        pairs += [(p * 16 + a, p * 16 + b) for a, b in along]
    return pairs


def core_swap():
    return [(i, i ^ 1) for i in range(8)]


def cost(us):
    return pl.CostEstimate(flops=0, transcendentals=0, bytes_accessed=int(us * 3.5e6))


def read_half(place_ref, window_ref, buffer, sem, parts=(0, 1, 2, 3)):
    copies = []
    for m, n in enumerate(parts):
        part = place_ref[0] * 4 + lax.rem(place_ref[1] + n, 4)
        rows = pl.ds(pl.multiple_of(part * PART, PART), PART)
        copies.append(pltpu.make_async_copy(window_ref.at[rows, pl.ds(0, NB)], buffer.at[m], sem.at[m]))
    return copies


def cast_half(window, half, first):
    def body(place_ref, window_ref, out_ref, buffer, sem):
        copies = read_half(place_ref, window_ref, buffer, sem)
        for copy in copies:
            copy.start()
        for n in range(4):
            copies[n].wait()
            out_ref[n * PART : (n + 1) * PART, :] = buffer[n].astype(BF16)

    return pl.pallas_call(
        body,
        in_specs=[SMEM, HBM],
        out_specs=VMEM,
        out_shape=jax.ShapeDtypeStruct((4 * PART, NB), BF16),
        scratch_shapes=[pltpu.VMEM((4, PART, NB), F32), pltpu.SemaphoreType.DMA((4,))],
        compiler_params=params(),
        cost_estimate=cost(2.0),
        name="cast_half",
    )(jnp.stack([half, first]).astype(jnp.int32), window)


def pair_up(window, half, first, partners, parts):
    count = len(parts)

    def body(place_ref, window_ref, partners_ref, *refs):
        outs, buffer, paired, sem = refs[:count], refs[count], refs[count + 1], refs[count + 2]
        copies = read_half(place_ref, window_ref, buffer, sem, parts)
        for copy in copies:
            copy.start()
        writes = [pltpu.make_async_copy(paired.at[m], outs[m], sem.at[count + m]) for m in range(count)]
        for m, n in enumerate(parts):
            paired[m, PART:, :] = partners_ref[n * PART : (n + 1) * PART, :]
        for m in range(count):
            copies[m].wait()
            paired[m, :PART, :] = buffer[m].astype(BF16)
            writes[m].start()
        for write in writes:
            write.wait()

    return pl.pallas_call(
        body,
        in_specs=[SMEM, HBM, VMEM],
        out_specs=[ANY] * count,
        out_shape=[jax.ShapeDtypeStruct((2 * PART, NB), BF16)] * count,
        scratch_shapes=[
            pltpu.VMEM((count, PART, NB), F32),
            pltpu.VMEM((count, 2 * PART, NB), BF16),
            pltpu.SemaphoreType.DMA((2 * count,)),
        ],
        compiler_params=params(),
        cost_estimate=cost(1.0 + 0.4 * count),
        name="pair_up",
    )(jnp.stack([half, first]).astype(jnp.int32), window, partners)


def pick(choice, arrays, order):
    choice = jnp.where(choice == 0, 0, sum(jnp.where(choice == s, n + 1, 0) for n, s in enumerate(order)))
    return jnp.where(
        choice < 2, jnp.where(choice == 0, arrays[0], arrays[1]), jnp.where(choice == 2, arrays[2], arrays[3])
    )


def factor(places, tiles):
    block_rows = 16

    def across(one, two):
        return lax.dot_general(one, two, (((0,), (0,)), ((), ())), preferred_element_type=F32)

    def body(places_ref, *refs):
        low_ref, inv_ref, weights_ref, work, stack, rows = refs[4:]
        for n in range(4):
            stack[n * 6 * NB : (n + 1) * 6 * NB, :] = refs[n][...]

        def tile_at(n):
            return stack[pl.ds(pl.multiple_of(places_ref[n] * NB, NB), NB), :]

        t = tile_at(0).astype(F32)
        row = lax.broadcasted_iota(jnp.int32, (NB, NB), 0)
        col = lax.broadcasted_iota(jnp.int32, (NB, NB), 1)
        work[:, :NB] = 0.5 * (t + t.T)
        work[:, NB:] = jnp.where(row == col, 1.0, 0.0)
        sub = lax.broadcasted_iota(jnp.int32, (block_rows, NB), 0)
        upper = []
        inverse = []
        for b in range(NB // block_rows):
            base = block_rows * b
            left = work[base : base + block_rows, :NB]
            right = work[base : base + block_rows, NB:]
            columns = [
                jnp.broadcast_to(left[:, base + s : base + s + 1], (block_rows, NB)) for s in range(block_rows)
            ]
            done_left = left
            done_right = right
            for s in range(block_rows):
                scale = lax.rsqrt(columns[s][s : s + 1, :])
                weight = columns[s] * scale
                for r in range(s + 1, block_rows):
                    columns[r] = columns[r] - weight * weight[r : r + 1, :]
                below = jnp.where(sub > s, weight, 0.0)
                line_left = left[s : s + 1, :] * scale
                line_right = right[s : s + 1, :] * scale
                done_left = jnp.where(sub == s, line_left, done_left)
                done_right = jnp.where(sub == s, line_right, done_right)
                left = left - below * line_left
                right = right - below * line_right
            upper.append(done_left)
            inverse.append(done_right)
            if base + block_rows < NB:
                done = jnp.concatenate([done_left, done_right], 1)
                high = done.astype(BF16)
                rest = (done - high.astype(F32)).astype(BF16)
                change = across(high[:, :NB], high) + across(high[:, :NB], rest) + across(rest[:, :NB], high)
                work[...] -= change
        up = jnp.concatenate(upper, 0)
        low_ref[...] = jnp.where(row >= col, up.T, 0.0)
        inv = jnp.where(row >= col, jnp.concatenate(inverse, 0), 0.0)
        inv_ref[...] = inv
        both = lax.dot_general(inv, inv, (((0,), (0,)), ((), ())), precision=HI, preferred_element_type=F32)
        high = both.astype(BF16)
        rest = (both - high.astype(F32)).astype(BF16)
        for n in range(1, LOOK + 1):
            row = places_ref[n] * NB + places_ref[2 * LOOK + 1] * SHARE
            place = pl.multiple_of(places_ref[LOOK + n] * SHARE, SHARE)
            rows[pl.ds(place, SHARE), :] = stack[pl.ds(pl.multiple_of(row, SHARE), SHARE), :]
        full = lax.dot_general(rows[...], high, (((1,), (0,)), ((), ())), preferred_element_type=F32)
        full += lax.dot_general(rows[...], rest, (((1,), (0,)), ((), ())), preferred_element_type=F32)
        weights_ref[...] = full.astype(BF16)

    return pl.pallas_call(
        body,
        in_specs=[SMEM] + [VMEM] * 4,
        out_specs=[VMEM] * 3,
        out_shape=[
            jax.ShapeDtypeStruct((NB, NB), F32),
            jax.ShapeDtypeStruct((NB, NB), F32),
            jax.ShapeDtypeStruct((LOOK * SHARE, NB), BF16),
        ],
        scratch_shapes=[pltpu.VMEM((NB, 2 * NB), F32), pltpu.VMEM((24 * NB, NB), BF16), pltpu.VMEM((LOOK * SHARE, NB), BF16)],
        compiler_params=params(),
        cost_estimate=cost(10.0),
        name="factor",
    )(places, *tiles)


def column_copies(source, buffer, target, lane, sem, count):
    size = buffer.shape[0] // count
    lanes = pl.ds(pl.multiple_of(lane * NB, NB), NB)
    into, out = [], []
    for n in range(count):
        rows = pl.ds(n * size, size)
        into.append(pltpu.make_async_copy(source.at[rows, lanes], buffer.at[rows], sem.at[0, n]))
        out.append(pltpu.make_async_copy(buffer.at[rows], target.at[rows, lanes], sem.at[1, n]))
    return into, out


def keep_column(scalars, window):
    def body(s_ref, window_ref, out_ref, buffer, sem):
        @pl.when(s_ref[2] == 0)
        def _():
            into, out = column_copies(window_ref, buffer, out_ref, 1 - s_ref[3], sem, 4)
            for copy in into:
                copy.start()
            for first, second in zip(into, out):
                first.wait()
                second.start()
            for copy in out:
                copy.wait()

    return pl.pallas_call(
        body,
        in_specs=[SMEM, HBM],
        out_specs=HBM,
        out_shape=jax.ShapeDtypeStruct(window.shape, F32),
        scratch_shapes=[pltpu.VMEM((window.shape[0], NB), F32), pltpu.SemaphoreType.DMA((2, 4))],
        compiler_params=params(),
        cost_estimate=cost(5.5),
        name="keep_column",
    )(scalars, window)


def write_panel(scalars, window, low, inv, out):
    count = 4
    size = window.shape[0] // count

    def body(s_ref, window_ref, low_ref, inv_ref, _, out_ref, buffer, sem):
        k, p = s_ref[0], s_ref[1]

        @pl.when(s_ref[2] == 1)
        def _():
            into, out = column_copies(window_ref, buffer, out_ref, 0, sem, count)
            for copy in into:
                copy.start()
            high = inv_ref[...].astype(BF16)
            for n in range(count):
                into[n].wait()
                if n == 0:
                    head = buffer[0 : 2 * NB, :]
                for t in range(size // 256):
                    rows = slice(n * size + t * 256, n * size + (t + 1) * 256)
                    buffer[rows, :] = lax.dot_general(
                        buffer[rows, :].astype(BF16), high, (((1,), (1,)), ((), ())), preferred_element_type=F32
                    )
                if n == 0:
                    for slot in range(2):
                        tile = slot * 8 + p
                        rows = pl.ds(slot * NB, NB)

                        @pl.when(tile == k)
                        def _():
                            buffer[rows, :] = low_ref[...]

                        @pl.when(tile < k)
                        def _():
                            buffer[rows, :] = head[slot * NB : (slot + 1) * NB, :]

                out[n].start()
            for copy in out:
                copy.wait()

    return pl.pallas_call(
        body,
        in_specs=[SMEM, HBM, VMEM, VMEM, HBM],
        out_specs=HBM,
        out_shape=jax.ShapeDtypeStruct(window.shape, F32),
        scratch_shapes=[pltpu.VMEM((window.shape[0], NB), F32), pltpu.SemaphoreType.DMA((2, count))],
        input_output_aliases={4: 0},
        compiler_params=params(),
        cost_estimate=cost(1.0),
        name="write_panel",
    )(scalars, window, low, inv, out)


def update(scalars, window, weights, parts, places, out):
    n = len(parts)
    size = PART // 2
    blocks = [(m, i) for m in range(n) for i in range(2)]
    s_all = jnp.concatenate([scalars, jnp.stack(places).astype(jnp.int32)])

    def body(s_ref, window_ref, weight_ref, *refs):
        panels, out_ref = refs[:n], refs[n + 1]
        buffer, sem = refs[n + 2 :]
        p, j = s_ref[1], s_ref[4]
        lanes = pl.ds(pl.multiple_of(s_ref[3] * NB, NB), NB)

        def rows(m, i):
            return pl.ds(pl.multiple_of(s_ref[5 + m] * PART + i * size, size), size)

        def read(m, i):
            return pltpu.make_async_copy(window_ref.at[rows(m, i), lanes], buffer.at[m, i], sem.at[0, m, i])

        def write(m, i):
            return pltpu.make_async_copy(buffer.at[m, i], out_ref.at[rows(m, i), lanes], sem.at[1, m, i])

        for m, i in blocks:
            read(m, i).start()
        for m, i in blocks:
            read(m, i).wait()
            for t in range(size // 256):
                change = lax.dot_general(
                    panels[m][i * size + t * 256 : i * size + (t + 1) * 256, :],
                    weight_ref[...],
                    (((1,), (1,)), ((), ())),
                    preferred_element_type=F32,
                )
                for u in range(2):
                    at = t * 256 + u * NB
                    tile = (s_ref[5 + m] * (PART // NB) + (i * size + at) // NB) * 8 + p
                    old = buffer[m, i, at : at + NB, :]
                    buffer[m, i, at : at + NB, :] = old - jnp.where(tile >= j, change[u * NB : (u + 1) * NB, :], 0.0)
            write(m, i).start()
        for m, i in blocks:
            write(m, i).wait()

    return pl.pallas_call(
        body,
        in_specs=[SMEM, HBM, VMEM] + [VMEM] * n + [HBM],
        out_specs=HBM,
        out_shape=jax.ShapeDtypeStruct(window.shape, F32),
        scratch_shapes=[
            pltpu.VMEM((n, 2, size, NB), F32),
            pltpu.SemaphoreType.DMA((2, n, 2)),
        ],
        input_output_aliases={3 + n: 0},
        compiler_params=params(),
        cost_estimate=cost(1.0 + 0.8 * n),
        name="update",
    )(s_all, window, weights, *parts, out)


def turn(s):
    return [(n * 2 + c, (n + (s if c == 0 else -s)) % 4 * 2 + c) for n in range(4) for c in range(2)]


def stage(arrays, axis, order):
    return [arrays[0]] + [lax.ppermute(arrays[s], BOTH, split_shift(s, axis)) for s in order]


def side_by_side(block, partner, c):
    return jnp.where(c == 0, jnp.concatenate([block, partner]), jnp.concatenate([partner, block]))


def send_rows(block, pair):
    return jnp.concatenate([lax.ppermute(pair, "prow", turn(1)), lax.ppermute(block, "prow", x_shift(2))])


def over_rows(pair, got, c):
    n = pair.shape[0] // 2
    other = lax.ppermute(got, "prow", core_swap())
    beside, across = got[: 2 * n], got[2 * n :]
    far = jnp.where(c == 0, jnp.concatenate([across, other[2 * n :]]), jnp.concatenate([other[2 * n :], across]))
    one = jnp.where(c == 0, beside, other[: 2 * n])
    three = jnp.where(c == 0, other[: 2 * n], beside)
    return [pair, one, far, three]


def body(window, panel_index):
    k = panel_index[0]
    p = lax.axis_index("prow")
    q = lax.axis_index("pcol")
    z, y = q // 4, q % 4
    x, c = p // 2, p % 2
    z0, y0 = k // 4, k % 4
    dz, dy = (z - z0) % 4, (y - y0) % 4
    slot = jnp.where(q <= k, 1, 0)
    j = slot * 16 + q
    scalars = jnp.stack([k, p, jnp.where(q == k, 1, 0), slot, j]).astype(jnp.int32)

    along, across = jnp.where(c == 0, z, y), jnp.where(c == 0, y, z)
    d_along, d_across = jnp.where(c == 0, dz, dy), jnp.where(c == 0, dy, dz)
    others = lax.ppermute(cast_half(window, 1 - c, across), "prow", core_swap())
    own = lax.dynamic_slice(window, (k // 8 * NB, 0), (3 * NB, NB)).astype(BF16)
    partner = lax.ppermute(own, "prow", core_swap())
    partner, others = lax.optimization_barrier((partner, others))
    messages = pair_up(window, c, along, others, (1, 2, 3))
    messages, own, partner, others, keep_scalars = lax.optimization_barrier((messages, own, partner, others, scalars))
    messages = pair_up(window, c, along, others, (0,)) + messages

    moved = stage(messages, 0, ORDER[0])
    pair = side_by_side(own, partner, c)
    got = send_rows(own, pair)
    out = keep_column(keep_scalars, window)
    moved, got, out = lax.optimization_barrier((moved, got, out))
    message = pick(d_along, moved, ORDER[0])

    message, got = lax.optimization_barrier((message, got))

    tiles = over_rows(pair, got, c)
    look = k + jnp.arange(LOOK + 1)
    at = (x - look % 8 // 2) % 4 * 6 + look % 2 * 3 + look // 8 - k // 8
    places = jnp.concatenate([at, look[1:] % 16, jnp.reshape(c, (1,))])
    low, inv, weights = factor(places.astype(jnp.int32), tiles)
    late, weights = lax.optimization_barrier((message, weights))
    moved = stage([message, message, late, message], 1, ORDER[1])
    weights = lax.all_to_all(weights, "pcol", 0, 0, tiled=True)
    out = write_panel(scalars, window, low, inv, out)
    moved, weights, out = lax.optimization_barrier((moved, weights, out))
    message = pick(d_across, moved, ORDER[1])

    message, weights = lax.optimization_barrier((message, weights))
    mine = message[:PART]
    other = lax.ppermute(message[PART:], "prow", core_swap())
    first = stage([mine] * 4, 0, ORDER[2])
    second = stage([other] * 4, 1, ORDER[3])
    places = [4 * c + (along - s) % 4 for s in (0,) + ORDER[2]] + [4 * (1 - c) + (across - s) % 4 for s in (0,) + ORDER[3]]

    weights = lax.dynamic_slice(weights, (k * SHARE, 0), (SHARE, NB))
    weights = side_by_side(weights, lax.ppermute(weights, "prow", core_swap()), c)
    out = update(scalars, window, weights, [mine, other], places[::4], out)
    first, second, out = lax.optimization_barrier((first, second, out))
    return update(scalars, window, weights, first[1:] + second[1:], places[1:4] + places[5:], out)


def solution(mesh):
    return jax.shard_map(
        body,
        mesh=mesh,
        in_specs=(P("prow", "pcol"), P()),
        out_specs=P("prow", "pcol"),
        check_vma=False,
    )
```

```python
import jax
import jax.numpy as jnp
from jax import lax
from jax.experimental import pallas as pl
from jax.experimental.pallas import tpu as pltpu
from jax.sharding import PartitionSpec as P

NB = 128
LOOK = 16
ORDER = ((1, 3, 2), (2, 3, 1), (1, 3, 2), (1, 3, 2))
VMEM_LIMIT = 20 * 1024 * 1024
F32 = jnp.float32
BF16 = jnp.bfloat16
HI = lax.Precision.HIGHEST
ANY = pl.BlockSpec(memory_space=pl.ANY)
HBM = pl.BlockSpec(memory_space=pltpu.HBM)
SMEM = pl.BlockSpec(memory_space=pltpu.SMEM)
VMEM = pl.BlockSpec(memory_space=pltpu.VMEM)
SHARE = 64
PART = 1536
BOTH = ("prow", "pcol")


def params():
    return pltpu.CompilerParams(vmem_limit_bytes=VMEM_LIMIT)


def z_shift(s):
    return [(z * 4 + y, (z + s) % 4 * 4 + y) for z in range(4) for y in range(4)]


def y_shift(s):
    return [(z * 4 + y, z * 4 + (y + s) % 4) for z in range(4) for y in range(4)]


def x_shift(s):
    return [(x * 2 + c, (x + s) % 4 * 2 + c) for x in range(4) for c in range(2)]


def split_shift(s, axis):
    pairs = []
    for p in range(8):
        along = z_shift(s) if (p + axis) % 2 == 0 else y_shift(s)
        pairs += [(p * 16 + a, p * 16 + b) for a, b in along]
    return pairs


def core_swap():
    return [(i, i ^ 1) for i in range(8)]


def cost(us):
    return pl.CostEstimate(flops=0, transcendentals=0, bytes_accessed=int(us * 3.5e6))


def read_half(place_ref, window_ref, buffer, sem, parts=(0, 1, 2, 3)):
    copies = []
    for m, n in enumerate(parts):
        part = place_ref[0] * 4 + lax.rem(place_ref[1] + n, 4)
        rows = pl.ds(pl.multiple_of(part * PART, PART), PART)
        copies.append(pltpu.make_async_copy(window_ref.at[rows, pl.ds(0, NB)], buffer.at[m], sem.at[m]))
    return copies


def in_hbm(array):
    return pltpu.with_memory_space_constraint(array, pltpu.HBM)


def cast_half(window, half, first):
    def body(place_ref, window_ref, out_ref, buffer, sem):
        copies = read_half(place_ref, window_ref, buffer, sem)
        for copy in copies:
            copy.start()
        for n in range(4):
            copies[n].wait()
            out_ref[n * PART : (n + 1) * PART, :] = buffer[n].astype(BF16)

    return pl.pallas_call(
        body,
        in_specs=[SMEM, HBM],
        out_specs=VMEM,
        out_shape=jax.ShapeDtypeStruct((4 * PART, NB), BF16),
        scratch_shapes=[pltpu.VMEM((4, PART, NB), F32), pltpu.SemaphoreType.DMA((4,))],
        compiler_params=params(),
        cost_estimate=cost(2.0),
        name="cast_half",
    )(jnp.stack([half, first]).astype(jnp.int32), in_hbm(window))


def pair_up(window, half, first, partners, parts):
    count = len(parts)

    def body(place_ref, window_ref, partners_ref, *refs):
        outs, buffer, paired, sem = refs[:count], refs[count], refs[count + 1], refs[count + 2]
        copies = read_half(place_ref, window_ref, buffer, sem, parts)
        for copy in copies:
            copy.start()
        writes = [pltpu.make_async_copy(paired.at[m], outs[m], sem.at[count + m]) for m in range(count)]
        for m, n in enumerate(parts):
            paired[m, PART:, :] = partners_ref[n * PART : (n + 1) * PART, :]
        for m in range(count):
            copies[m].wait()
            paired[m, :PART, :] = buffer[m].astype(BF16)
            writes[m].start()
        for write in writes:
            write.wait()

    return pl.pallas_call(
        body,
        in_specs=[SMEM, HBM, VMEM],
        out_specs=[ANY] * count,
        out_shape=[jax.ShapeDtypeStruct((2 * PART, NB), BF16)] * count,
        scratch_shapes=[
            pltpu.VMEM((count, PART, NB), F32),
            pltpu.VMEM((count, 2 * PART, NB), BF16),
            pltpu.SemaphoreType.DMA((2 * count,)),
        ],
        compiler_params=params(),
        cost_estimate=cost(1.0 + 0.4 * count),
        name="pair_up",
    )(jnp.stack([half, first]).astype(jnp.int32), in_hbm(window), partners)


def pick(choice, arrays, order):
    choice = jnp.where(choice == 0, 0, sum(jnp.where(choice == s, n + 1, 0) for n, s in enumerate(order)))
    return jnp.where(
        choice < 2, jnp.where(choice == 0, arrays[0], arrays[1]), jnp.where(choice == 2, arrays[2], arrays[3])
    )


def take(choice, arrays, order):
    def body(choice_ref, *refs):
        for n, s in enumerate((0,) + order):

            @pl.when(choice_ref[0] == s)
            def _():
                refs[4][...] = refs[n][...]

    return pl.pallas_call(
        body,
        in_specs=[SMEM] + [VMEM] * 4,
        out_specs=VMEM,
        out_shape=jax.ShapeDtypeStruct(arrays[0].shape, BF16),
        compiler_params=params(),
        cost_estimate=cost(0.5),
        name="take",
    )(jnp.reshape(choice, (1,)).astype(jnp.int32), *arrays)


def factor(places, tiles):
    block_rows = 16

    def across(one, two):
        return lax.dot_general(one, two, (((0,), (0,)), ((), ())), preferred_element_type=F32)

    def body(places_ref, *refs):
        low_ref, inv_ref, weights_ref, work, stack, rows = refs[4:]
        for n in range(4):
            stack[n * 6 * NB : (n + 1) * 6 * NB, :] = refs[n][...]

        def tile_at(n):
            return stack[pl.ds(pl.multiple_of(places_ref[n] * NB, NB), NB), :]

        t = tile_at(0).astype(F32)
        row = lax.broadcasted_iota(jnp.int32, (NB, NB), 0)
        col = lax.broadcasted_iota(jnp.int32, (NB, NB), 1)
        work[:, :NB] = 0.5 * (t + t.T)
        work[:, NB:] = jnp.where(row == col, 1.0, 0.0)
        sub = lax.broadcasted_iota(jnp.int32, (block_rows, NB), 0)
        upper = []
        inverse = []
        for b in range(NB // block_rows):
            base = block_rows * b
            left = work[base : base + block_rows, :NB]
            right = work[base : base + block_rows, NB:]
            columns = [
                jnp.broadcast_to(left[:, base + s : base + s + 1], (block_rows, NB)) for s in range(block_rows)
            ]
            done_left = left
            done_right = right
            for s in range(block_rows):
                scale = lax.rsqrt(columns[s][s : s + 1, :])
                weight = columns[s] * scale
                for r in range(s + 1, block_rows):
                    columns[r] = columns[r] - weight * weight[r : r + 1, :]
                below = jnp.where(sub > s, weight, 0.0)
                line_left = left[s : s + 1, :] * scale
                line_right = right[s : s + 1, :] * scale
                done_left = jnp.where(sub == s, line_left, done_left)
                done_right = jnp.where(sub == s, line_right, done_right)
                left = left - below * line_left
                right = right - below * line_right
            upper.append(done_left)
            inverse.append(done_right)
            if base + block_rows < NB:
                done = jnp.concatenate([done_left, done_right], 1)
                high = done.astype(BF16)
                rest = (done - high.astype(F32)).astype(BF16)
                change = across(high[:, :NB], high) + across(high[:, :NB], rest) + across(rest[:, :NB], high)
                work[...] -= change
        up = jnp.concatenate(upper, 0)
        low_ref[...] = jnp.where(row >= col, up.T, 0.0)
        inv = jnp.where(row >= col, jnp.concatenate(inverse, 0), 0.0)
        inv_ref[...] = inv
        both = lax.dot_general(inv, inv, (((0,), (0,)), ((), ())), precision=HI, preferred_element_type=F32)
        high = both.astype(BF16)
        rest = (both - high.astype(F32)).astype(BF16)
        for n in range(1, LOOK + 1):
            row = places_ref[n] * NB + places_ref[2 * LOOK + 1] * SHARE
            place = pl.multiple_of(places_ref[LOOK + n] * SHARE, SHARE)
            rows[pl.ds(place, SHARE), :] = stack[pl.ds(pl.multiple_of(row, SHARE), SHARE), :]
        full = lax.dot_general(rows[...], high, (((1,), (0,)), ((), ())), preferred_element_type=F32)
        full += lax.dot_general(rows[...], rest, (((1,), (0,)), ((), ())), preferred_element_type=F32)
        weights_ref[...] = full.astype(BF16)

    return pl.pallas_call(
        body,
        in_specs=[SMEM] + [VMEM] * 4,
        out_specs=[VMEM] * 3,
        out_shape=[
            jax.ShapeDtypeStruct((NB, NB), F32),
            jax.ShapeDtypeStruct((NB, NB), F32),
            jax.ShapeDtypeStruct((LOOK * SHARE, NB), BF16),
        ],
        scratch_shapes=[pltpu.VMEM((NB, 2 * NB), F32), pltpu.VMEM((24 * NB, NB), BF16), pltpu.VMEM((LOOK * SHARE, NB), BF16)],
        compiler_params=params(),
        cost_estimate=cost(10.0),
        name="factor",
    )(places, *tiles)


def column_copies(source, buffer, target, lane, sem, count):
    size = buffer.shape[0] // count
    lanes = pl.ds(pl.multiple_of(lane * NB, NB), NB)
    into, out = [], []
    for n in range(count):
        rows = pl.ds(n * size, size)
        into.append(pltpu.make_async_copy(source.at[rows, lanes], buffer.at[rows], sem.at[0, n]))
        out.append(pltpu.make_async_copy(buffer.at[rows], target.at[rows, lanes], sem.at[1, n]))
    return into, out


def keep_column(scalars, window):
    def body(s_ref, window_ref, out_ref, buffer, sem):
        @pl.when(s_ref[2] == 0)
        def _():
            into, out = column_copies(window_ref, buffer, out_ref, 1 - s_ref[3], sem, 4)
            for copy in into:
                copy.start()
            for first, second in zip(into, out):
                first.wait()
                second.start()
            for copy in out:
                copy.wait()

    return pl.pallas_call(
        body,
        in_specs=[SMEM, HBM],
        out_specs=HBM,
        out_shape=jax.ShapeDtypeStruct(window.shape, F32),
        scratch_shapes=[pltpu.VMEM((window.shape[0], NB), F32), pltpu.SemaphoreType.DMA((2, 4))],
        compiler_params=params(),
        cost_estimate=cost(5.5),
        name="keep_column",
    )(scalars, in_hbm(window))


def write_panel(scalars, window, low, inv, out):
    count = 4
    size = window.shape[0] // count

    def body(s_ref, window_ref, low_ref, inv_ref, _, out_ref, buffer, sem):
        k, p = s_ref[0], s_ref[1]

        @pl.when(s_ref[2] == 1)
        def _():
            into, out = column_copies(window_ref, buffer, out_ref, 0, sem, count)
            for copy in into:
                copy.start()
            high = inv_ref[...].astype(BF16)
            for n in range(count):
                into[n].wait()
                if n == 0:
                    head = buffer[0 : 2 * NB, :]
                for t in range(size // 256):
                    rows = slice(n * size + t * 256, n * size + (t + 1) * 256)
                    buffer[rows, :] = lax.dot_general(
                        buffer[rows, :].astype(BF16), high, (((1,), (1,)), ((), ())), preferred_element_type=F32
                    )
                if n == 0:
                    for slot in range(2):
                        tile = slot * 8 + p
                        rows = pl.ds(slot * NB, NB)

                        @pl.when(tile == k)
                        def _():
                            buffer[rows, :] = low_ref[...]

                        @pl.when(tile < k)
                        def _():
                            buffer[rows, :] = head[slot * NB : (slot + 1) * NB, :]

                out[n].start()
            for copy in out:
                copy.wait()

    return pl.pallas_call(
        body,
        in_specs=[SMEM, HBM, VMEM, VMEM, HBM],
        out_specs=HBM,
        out_shape=jax.ShapeDtypeStruct(window.shape, F32),
        scratch_shapes=[pltpu.VMEM((window.shape[0], NB), F32), pltpu.SemaphoreType.DMA((2, count))],
        input_output_aliases={4: 0},
        compiler_params=params(),
        cost_estimate=cost(1.0),
        name="write_panel",
    )(scalars, in_hbm(window), low, inv, out)


def update(scalars, window, weights, parts, places, out, ahead=(), held=None):
    n, more = len(parts), len(ahead)
    size = PART // 2
    blocks = [(m, i) for m in range(n) for i in range(2)]
    s_all = jnp.concatenate([scalars, jnp.stack(list(places) + list(ahead)).astype(jnp.int32)])

    def body(s_ref, source_ref, weight_ref, *refs):
        panels, out_ref = refs[:n], refs[n + 1]
        buffer, sem, ahead_sem = refs[-3:]
        p, j = s_ref[1], s_ref[4]
        lanes = pl.ds(pl.multiple_of(s_ref[3] * NB, NB), NB)
        reads_ahead = [
            pltpu.make_async_copy(
                source_ref.at[pl.ds(pl.multiple_of(s_ref[5 + n + m] * PART, PART), PART), lanes],
                refs[n + 2].at[m],
                ahead_sem.at[m],
            )
            for m in range(more)
        ]

        def rows(m, i):
            return pl.ds(pl.multiple_of(s_ref[5 + m] * PART + i * size, size), size)

        def read(m, i):
            return pltpu.make_async_copy(source_ref.at[rows(m, i), lanes], buffer.at[m, i], sem.at[0, m, i])

        def write(m, i):
            return pltpu.make_async_copy(buffer.at[m, i], out_ref.at[rows(m, i), lanes], sem.at[1, m, i])

        if held is None:
            for m, i in blocks:
                read(m, i).start()
        for copy in reads_ahead:
            copy.start()
        for m, i in blocks:
            if held is None:
                read(m, i).wait()
            for t in range(size // 256):
                change = lax.dot_general(
                    panels[m][i * size + t * 256 : i * size + (t + 1) * 256, :],
                    weight_ref[...],
                    (((1,), (1,)), ((), ())),
                    preferred_element_type=F32,
                )
                for u in range(2):
                    at = t * 256 + u * NB
                    tile = (s_ref[5 + m] * (PART // NB) + (i * size + at) // NB) * 8 + p
                    if held is None:
                        old = buffer[m, i, at : at + NB, :]
                    else:
                        old = source_ref[m, i * size + at : i * size + at + NB, :]
                    buffer[m, i, at : at + NB, :] = old - jnp.where(tile >= j, change[u * NB : (u + 1) * NB, :], 0.0)
            write(m, i).start()
        for m, i in blocks:
            write(m, i).wait()
        for copy in reads_ahead:
            copy.wait()

    given = pl.pallas_call(
        body,
        in_specs=[SMEM, HBM if held is None else VMEM, VMEM] + [VMEM] * n + [HBM],
        out_specs=[HBM] + [VMEM] * min(more, 1),
        out_shape=[jax.ShapeDtypeStruct(window.shape, F32)]
        + [jax.ShapeDtypeStruct((more, PART, NB), F32)] * min(more, 1),
        scratch_shapes=[
            pltpu.VMEM((n, 2, size, NB), F32),
            pltpu.SemaphoreType.DMA((2, n, 2)),
            pltpu.SemaphoreType.DMA((max(more, 1),)),
        ],
        input_output_aliases={3 + n: 0},
        compiler_params=params(),
        cost_estimate=cost(1.0 + 0.8 * n),
        name="update",
    )(s_all, in_hbm(window) if held is None else held, weights, *parts, out)
    return given if more else given[0]


def turn(s):
    return [(n * 2 + c, (n + (s if c == 0 else -s)) % 4 * 2 + c) for n in range(4) for c in range(2)]


def stage(arrays, axis, order):
    return [arrays[0]] + [lax.ppermute(arrays[s], BOTH, split_shift(s, axis)) for s in order]


def side_by_side(block, partner, c):
    return jnp.where(c == 0, jnp.concatenate([block, partner]), jnp.concatenate([partner, block]))


def send_rows(block, pair):
    return jnp.concatenate([lax.ppermute(pair, "prow", turn(1)), lax.ppermute(block, "prow", x_shift(2))])


def over_rows(pair, got, c):
    n = pair.shape[0] // 2
    other = lax.ppermute(got, "prow", core_swap())
    beside, across = got[: 2 * n], got[2 * n :]
    far = jnp.where(c == 0, jnp.concatenate([across, other[2 * n :]]), jnp.concatenate([other[2 * n :], across]))
    one = jnp.where(c == 0, beside, other[: 2 * n])
    three = jnp.where(c == 0, other[: 2 * n], beside)
    return [pair, one, far, three]


def body(window, panel_index):
    k = panel_index[0]
    p = lax.axis_index("prow")
    q = lax.axis_index("pcol")
    z, y = q // 4, q % 4
    x, c = p // 2, p % 2
    z0, y0 = k // 4, k % 4
    dz, dy = (z - z0) % 4, (y - y0) % 4
    slot = jnp.where(q <= k, 1, 0)
    j = slot * 16 + q
    scalars = jnp.stack([k, p, jnp.where(q == k, 1, 0), slot, j]).astype(jnp.int32)

    along, across = jnp.where(c == 0, z, y), jnp.where(c == 0, y, z)
    d_along, d_across = jnp.where(c == 0, dz, dy), jnp.where(c == 0, dy, dz)
    others = lax.ppermute(cast_half(window, 1 - c, across), "prow", core_swap())
    own = lax.dynamic_slice(window, (k // 8 * NB, 0), (3 * NB, NB)).astype(BF16)
    partner = lax.ppermute(own, "prow", core_swap())
    partner, others = lax.optimization_barrier((partner, others))
    messages = pair_up(window, c, along, others, (1, 2, 3))
    messages, own, partner, others, keep_scalars = lax.optimization_barrier((messages, own, partner, others, scalars))
    messages = pair_up(window, c, along, others, (0,)) + messages

    moved = stage(messages, 0, ORDER[0])
    pair = side_by_side(own, partner, c)
    got = send_rows(own, pair)
    out = keep_column(keep_scalars, window)
    moved, got, out = lax.optimization_barrier((moved, got, out))
    message = take(d_along, moved, ORDER[0])

    message, got = lax.optimization_barrier((message, got))

    tiles = over_rows(pair, got, c)
    look = k + jnp.arange(LOOK + 1)
    at = (x - look % 8 // 2) % 4 * 6 + look % 2 * 3 + look // 8 - k // 8
    places = jnp.concatenate([at, look[1:] % 16, jnp.reshape(c, (1,))])
    low, inv, weights = factor(places.astype(jnp.int32), tiles)
    late, weights = lax.optimization_barrier((message, weights))
    moved = stage([message, message, late, message], 1, ORDER[1])
    weights = lax.all_to_all(weights, "pcol", 0, 0, tiled=True)
    out = write_panel(scalars, window, low, inv, out)
    moved, weights, out = lax.optimization_barrier((moved, weights, out))
    message = pick(d_across, moved, ORDER[1])

    message, weights = lax.optimization_barrier((message, weights))
    mine = message[:PART]
    other = lax.ppermute(message[PART:], "prow", core_swap())
    first = stage([mine] * 4, 0, ORDER[2])
    second = stage([other] * 4, 1, ORDER[3])
    places = [4 * c + (along - s) % 4 for s in (0,) + ORDER[2]] + [4 * (1 - c) + (across - s) % 4 for s in (0,) + ORDER[3]]

    weights = lax.dynamic_slice(weights, (k * SHARE, 0), (SHARE, NB))
    weights = side_by_side(weights, lax.ppermute(weights, "prow", core_swap()), c)
    later = places[1:4] + places[5:]
    out, held = update(scalars, window, weights, [mine, other], places[::4], out, ahead=later)
    first, second, out, held = lax.optimization_barrier((first, second, out, held))
    return update(scalars, window, weights, first[1:] + second[1:], later, out, held=held)


def solution(mesh):
    return jax.shard_map(
        body,
        mesh=mesh,
        in_specs=(P("prow", "pcol"), P()),
        out_specs=P("prow", "pcol"),
        check_vma=False,
    )
```

```python
import jax
import jax.numpy as jnp
from jax import lax
from jax.experimental import pallas as pl
from jax.experimental.pallas import tpu as pltpu
from jax.sharding import PartitionSpec as P

NB = 128
LOOK = 16
ORDER = ((1, 3, 2), (2, 3, 1), (1, 3, 2), (1, 3, 2))
VMEM_LIMIT = 20 * 1024 * 1024
F32 = jnp.float32
BF16 = jnp.bfloat16
HI = lax.Precision.HIGHEST
ANY = pl.BlockSpec(memory_space=pl.ANY)
HBM = pl.BlockSpec(memory_space=pltpu.HBM)
SMEM = pl.BlockSpec(memory_space=pltpu.SMEM)
VMEM = pl.BlockSpec(memory_space=pltpu.VMEM)
SHARE = 64
PART = 1536
BOTH = ("prow", "pcol")


def params():
    return pltpu.CompilerParams(vmem_limit_bytes=VMEM_LIMIT)


def z_shift(s):
    return [(z * 4 + y, (z + s) % 4 * 4 + y) for z in range(4) for y in range(4)]


def y_shift(s):
    return [(z * 4 + y, z * 4 + (y + s) % 4) for z in range(4) for y in range(4)]


def x_shift(s):
    return [(x * 2 + c, (x + s) % 4 * 2 + c) for x in range(4) for c in range(2)]


def split_shift(s, axis):
    pairs = []
    for p in range(8):
        along = z_shift(s) if (p + axis) % 2 == 0 else y_shift(s)
        pairs += [(p * 16 + a, p * 16 + b) for a, b in along]
    return pairs


def core_swap():
    return [(i, i ^ 1) for i in range(8)]


def cost(us):
    return pl.CostEstimate(flops=0, transcendentals=0, bytes_accessed=int(us * 3.5e6))


def read_half(place_ref, window_ref, buffer, sem, parts=(0, 1, 2, 3)):
    copies = []
    for m, n in enumerate(parts):
        part = place_ref[0] * 4 + lax.rem(place_ref[1] + n, 4)
        rows = pl.ds(pl.multiple_of(part * PART, PART), PART)
        copies.append(pltpu.make_async_copy(window_ref.at[rows, pl.ds(0, NB)], buffer.at[m], sem.at[m]))
    return copies


def in_hbm(array):
    return pltpu.with_memory_space_constraint(array, pltpu.HBM)


def cast_half(window, half, first):
    def body(place_ref, window_ref, out_ref, buffer, sem):
        copies = read_half(place_ref, window_ref, buffer, sem)
        for copy in copies:
            copy.start()
        for n in range(4):
            copies[n].wait()
            out_ref[n * PART : (n + 1) * PART, :] = buffer[n].astype(BF16)

    return pl.pallas_call(
        body,
        in_specs=[SMEM, HBM],
        out_specs=VMEM,
        out_shape=jax.ShapeDtypeStruct((4 * PART, NB), BF16),
        scratch_shapes=[pltpu.VMEM((4, PART, NB), F32), pltpu.SemaphoreType.DMA((4,))],
        compiler_params=params(),
        cost_estimate=cost(2.0),
        name="cast_half",
    )(jnp.stack([half, first]).astype(jnp.int32), in_hbm(window))


def pair_up(window, half, first, partners, parts):
    count = len(parts)

    def body(place_ref, window_ref, partners_ref, *refs):
        outs, buffer, paired, sem = refs[:count], refs[count], refs[count + 1], refs[count + 2]
        copies = read_half(place_ref, window_ref, buffer, sem, parts)
        for copy in copies:
            copy.start()
        writes = [pltpu.make_async_copy(paired.at[m], outs[m], sem.at[count + m]) for m in range(count)]
        for m, n in enumerate(parts):
            paired[m, PART:, :] = partners_ref[n * PART : (n + 1) * PART, :]
        for m in range(count):
            copies[m].wait()
            paired[m, :PART, :] = buffer[m].astype(BF16)
            writes[m].start()
        for write in writes:
            write.wait()

    return pl.pallas_call(
        body,
        in_specs=[SMEM, HBM, VMEM],
        out_specs=[ANY] * count,
        out_shape=[jax.ShapeDtypeStruct((2 * PART, NB), BF16)] * count,
        scratch_shapes=[
            pltpu.VMEM((count, PART, NB), F32),
            pltpu.VMEM((count, 2 * PART, NB), BF16),
            pltpu.SemaphoreType.DMA((2 * count,)),
        ],
        compiler_params=params(),
        cost_estimate=cost(1.0 + 0.4 * count),
        name="pair_up",
    )(jnp.stack([half, first]).astype(jnp.int32), in_hbm(window), partners)


def pick(choice, arrays, order):
    choice = jnp.where(choice == 0, 0, sum(jnp.where(choice == s, n + 1, 0) for n, s in enumerate(order)))
    return jnp.where(
        choice < 2, jnp.where(choice == 0, arrays[0], arrays[1]), jnp.where(choice == 2, arrays[2], arrays[3])
    )


def take(choice, arrays, order):
    def body(choice_ref, *refs):
        for n, s in enumerate((0,) + order):

            @pl.when(choice_ref[0] == s)
            def _():
                refs[4][...] = refs[n][...]

    return pl.pallas_call(
        body,
        in_specs=[SMEM] + [VMEM] * 4,
        out_specs=VMEM,
        out_shape=jax.ShapeDtypeStruct(arrays[0].shape, BF16),
        compiler_params=params(),
        cost_estimate=cost(0.5),
        name="take",
    )(jnp.reshape(choice, (1,)).astype(jnp.int32), *arrays)


def factor(places, tiles):
    block_rows = 16

    def across(one, two):
        return lax.dot_general(one, two, (((0,), (0,)), ((), ())), preferred_element_type=F32)

    def body(places_ref, *refs):
        low_ref, inv_ref, weights_ref, work, stack, rows = refs[4:]
        for n in range(4):
            stack[n * 6 * NB : (n + 1) * 6 * NB, :] = refs[n][...]

        def tile_at(n):
            return stack[pl.ds(pl.multiple_of(places_ref[n] * NB, NB), NB), :]

        t = tile_at(0).astype(F32)
        row = lax.broadcasted_iota(jnp.int32, (NB, NB), 0)
        col = lax.broadcasted_iota(jnp.int32, (NB, NB), 1)
        work[:, :NB] = 0.5 * (t + t.T)
        work[:, NB:] = jnp.where(row == col, 1.0, 0.0)
        sub = lax.broadcasted_iota(jnp.int32, (block_rows, NB), 0)
        upper = []
        inverse = []
        for b in range(NB // block_rows):
            base = block_rows * b
            left = work[base : base + block_rows, :NB]
            right = work[base : base + block_rows, NB:]
            columns = [
                jnp.broadcast_to(left[:, base + s : base + s + 1], (block_rows, NB)) for s in range(block_rows)
            ]
            done_left = left
            done_right = right
            for s in range(block_rows):
                scale = lax.rsqrt(columns[s][s : s + 1, :])
                weight = columns[s] * scale
                for r in range(s + 1, block_rows):
                    columns[r] = columns[r] - weight * weight[r : r + 1, :]
                below = jnp.where(sub > s, weight, 0.0)
                line_left = left[s : s + 1, :] * scale
                line_right = right[s : s + 1, :] * scale
                done_left = jnp.where(sub == s, line_left, done_left)
                done_right = jnp.where(sub == s, line_right, done_right)
                left = left - below * line_left
                right = right - below * line_right
            upper.append(done_left)
            inverse.append(done_right)
            if base + block_rows < NB:
                done = jnp.concatenate([done_left, done_right], 1)
                high = done.astype(BF16)
                rest = (done - high.astype(F32)).astype(BF16)
                left_sides = jnp.concatenate([high[:, :NB], high[:, :NB], rest[:, :NB]], 0)
                work[...] -= across(left_sides, jnp.concatenate([high, rest, high], 0))
        up = jnp.concatenate(upper, 0)
        low_ref[...] = jnp.where(row >= col, up.T, 0.0)
        inv = jnp.where(row >= col, jnp.concatenate(inverse, 0), 0.0)
        inv_ref[...] = inv
        both = lax.dot_general(inv, inv, (((0,), (0,)), ((), ())), precision=HI, preferred_element_type=F32)
        high = both.astype(BF16)
        rest = (both - high.astype(F32)).astype(BF16)
        for n in range(1, LOOK + 1):
            row = places_ref[n] * NB + places_ref[2 * LOOK + 1] * SHARE
            place = pl.multiple_of(places_ref[LOOK + n] * SHARE, SHARE)
            rows[pl.ds(place, SHARE), :] = stack[pl.ds(pl.multiple_of(row, SHARE), SHARE), :]
        twice = jnp.concatenate([rows[...], rows[...]], 1)
        full = lax.dot_general(
            twice, jnp.concatenate([high, rest], 0), (((1,), (0,)), ((), ())), preferred_element_type=F32
        )
        weights_ref[...] = full.astype(BF16)

    return pl.pallas_call(
        body,
        in_specs=[SMEM] + [VMEM] * 4,
        out_specs=[VMEM] * 3,
        out_shape=[
            jax.ShapeDtypeStruct((NB, NB), F32),
            jax.ShapeDtypeStruct((NB, NB), F32),
            jax.ShapeDtypeStruct((LOOK * SHARE, NB), BF16),
        ],
        scratch_shapes=[pltpu.VMEM((NB, 2 * NB), F32), pltpu.VMEM((24 * NB, NB), BF16), pltpu.VMEM((LOOK * SHARE, NB), BF16)],
        compiler_params=params(),
        cost_estimate=cost(10.0),
        name="factor",
    )(places, *tiles)


def column_copies(source, buffer, target, lane, sem, count):
    size = buffer.shape[0] // count
    lanes = pl.ds(pl.multiple_of(lane * NB, NB), NB)
    into, out = [], []
    for n in range(count):
        rows = pl.ds(n * size, size)
        into.append(pltpu.make_async_copy(source.at[rows, lanes], buffer.at[rows], sem.at[0, n]))
        out.append(pltpu.make_async_copy(buffer.at[rows], target.at[rows, lanes], sem.at[1, n]))
    return into, out


def keep_column(scalars, window):
    def body(s_ref, window_ref, out_ref, buffer, sem):
        @pl.when(s_ref[2] == 0)
        def _():
            into, out = column_copies(window_ref, buffer, out_ref, 1 - s_ref[3], sem, 4)
            for copy in into:
                copy.start()
            for first, second in zip(into, out):
                first.wait()
                second.start()
            for copy in out:
                copy.wait()

    return pl.pallas_call(
        body,
        in_specs=[SMEM, HBM],
        out_specs=HBM,
        out_shape=jax.ShapeDtypeStruct(window.shape, F32),
        scratch_shapes=[pltpu.VMEM((window.shape[0], NB), F32), pltpu.SemaphoreType.DMA((2, 4))],
        compiler_params=params(),
        cost_estimate=cost(5.5),
        name="keep_column",
    )(scalars, in_hbm(window))


def write_panel(scalars, window, low, inv, out):
    count = 4
    size = window.shape[0] // count

    def body(s_ref, window_ref, low_ref, inv_ref, _, out_ref, buffer, sem):
        k, p = s_ref[0], s_ref[1]

        @pl.when(s_ref[2] == 1)
        def _():
            into, out = column_copies(window_ref, buffer, out_ref, 0, sem, count)
            for copy in into:
                copy.start()
            high = inv_ref[...].astype(BF16)
            for n in range(count):
                into[n].wait()
                if n == 0:
                    head = buffer[0 : 2 * NB, :]
                for t in range(size // 256):
                    rows = slice(n * size + t * 256, n * size + (t + 1) * 256)
                    buffer[rows, :] = lax.dot_general(
                        buffer[rows, :].astype(BF16), high, (((1,), (1,)), ((), ())), preferred_element_type=F32
                    )
                if n == 0:
                    for slot in range(2):
                        tile = slot * 8 + p
                        rows = pl.ds(slot * NB, NB)

                        @pl.when(tile == k)
                        def _():
                            buffer[rows, :] = low_ref[...]

                        @pl.when(tile < k)
                        def _():
                            buffer[rows, :] = head[slot * NB : (slot + 1) * NB, :]

                out[n].start()
            for copy in out:
                copy.wait()

    return pl.pallas_call(
        body,
        in_specs=[SMEM, HBM, VMEM, VMEM, HBM],
        out_specs=HBM,
        out_shape=jax.ShapeDtypeStruct(window.shape, F32),
        scratch_shapes=[pltpu.VMEM((window.shape[0], NB), F32), pltpu.SemaphoreType.DMA((2, count))],
        input_output_aliases={4: 0},
        compiler_params=params(),
        cost_estimate=cost(1.0),
        name="write_panel",
    )(scalars, in_hbm(window), low, inv, out)


def update(scalars, window, weights, parts, places, out, ahead=(), held=None):
    n, more = len(parts), len(ahead)
    size = PART // 2
    blocks = [(m, i) for m in range(n) for i in range(2)]
    s_all = jnp.concatenate([scalars, jnp.stack(list(places) + list(ahead)).astype(jnp.int32)])

    def body(s_ref, source_ref, weight_ref, *refs):
        panels, out_ref = refs[:n], refs[n + 1]
        buffer, sem, ahead_sem = refs[-3:]
        p, j = s_ref[1], s_ref[4]
        lanes = pl.ds(pl.multiple_of(s_ref[3] * NB, NB), NB)
        reads_ahead = [
            pltpu.make_async_copy(
                source_ref.at[pl.ds(pl.multiple_of(s_ref[5 + n + m] * PART, PART), PART), lanes],
                refs[n + 2].at[m],
                ahead_sem.at[m],
            )
            for m in range(more)
        ]

        def rows(m, i):
            return pl.ds(pl.multiple_of(s_ref[5 + m] * PART + i * size, size), size)

        def read(m, i):
            return pltpu.make_async_copy(source_ref.at[rows(m, i), lanes], buffer.at[m, i], sem.at[0, m, i])

        def write(m, i):
            return pltpu.make_async_copy(buffer.at[m, i], out_ref.at[rows(m, i), lanes], sem.at[1, m, i])

        if held is None:
            for m, i in blocks:
                read(m, i).start()
        for copy in reads_ahead:
            copy.start()
        for m, i in blocks:
            if held is None:
                read(m, i).wait()
            for t in range(size // 256):
                change = lax.dot_general(
                    panels[m][i * size + t * 256 : i * size + (t + 1) * 256, :],
                    weight_ref[...],
                    (((1,), (1,)), ((), ())),
                    preferred_element_type=F32,
                )
                for u in range(2):
                    at = t * 256 + u * NB
                    tile = (s_ref[5 + m] * (PART // NB) + (i * size + at) // NB) * 8 + p
                    if held is None:
                        old = buffer[m, i, at : at + NB, :]
                    else:
                        old = source_ref[m, i * size + at : i * size + at + NB, :]
                    buffer[m, i, at : at + NB, :] = old - jnp.where(tile >= j, change[u * NB : (u + 1) * NB, :], 0.0)
            write(m, i).start()
        for m, i in blocks:
            write(m, i).wait()
        for copy in reads_ahead:
            copy.wait()

    given = pl.pallas_call(
        body,
        in_specs=[SMEM, HBM if held is None else VMEM, VMEM] + [VMEM] * n + [HBM],
        out_specs=[HBM] + [VMEM] * min(more, 1),
        out_shape=[jax.ShapeDtypeStruct(window.shape, F32)]
        + [jax.ShapeDtypeStruct((more, PART, NB), F32)] * min(more, 1),
        scratch_shapes=[
            pltpu.VMEM((n, 2, size, NB), F32),
            pltpu.SemaphoreType.DMA((2, n, 2)),
            pltpu.SemaphoreType.DMA((max(more, 1),)),
        ],
        input_output_aliases={3 + n: 0},
        compiler_params=params(),
        cost_estimate=cost(1.0 + 0.8 * n),
        name="update",
    )(s_all, in_hbm(window) if held is None else held, weights, *parts, out)
    return given if more else given[0]


def turn(s):
    return [(n * 2 + c, (n + (s if c == 0 else -s)) % 4 * 2 + c) for n in range(4) for c in range(2)]


def stage(arrays, axis, order):
    return [arrays[0]] + [lax.ppermute(arrays[s], BOTH, split_shift(s, axis)) for s in order]


def side_by_side(block, partner, c):
    return jnp.where(c == 0, jnp.concatenate([block, partner]), jnp.concatenate([partner, block]))


def send_rows(block, pair):
    return jnp.concatenate([lax.ppermute(pair, "prow", turn(1)), lax.ppermute(block, "prow", x_shift(2))])


def over_rows(pair, got, c):
    n = pair.shape[0] // 2
    other = lax.ppermute(got, "prow", core_swap())
    beside, across = got[: 2 * n], got[2 * n :]
    far = jnp.where(c == 0, jnp.concatenate([across, other[2 * n :]]), jnp.concatenate([other[2 * n :], across]))
    one = jnp.where(c == 0, beside, other[: 2 * n])
    three = jnp.where(c == 0, other[: 2 * n], beside)
    return [pair, one, far, three]


def body(window, panel_index):
    k = panel_index[0]
    p = lax.axis_index("prow")
    q = lax.axis_index("pcol")
    z, y = q // 4, q % 4
    x, c = p // 2, p % 2
    z0, y0 = k // 4, k % 4
    dz, dy = (z - z0) % 4, (y - y0) % 4
    slot = jnp.where(q <= k, 1, 0)
    j = slot * 16 + q
    scalars = jnp.stack([k, p, jnp.where(q == k, 1, 0), slot, j]).astype(jnp.int32)

    along, across = jnp.where(c == 0, z, y), jnp.where(c == 0, y, z)
    d_along, d_across = jnp.where(c == 0, dz, dy), jnp.where(c == 0, dy, dz)
    others = lax.ppermute(cast_half(window, 1 - c, across), "prow", core_swap())
    own = lax.dynamic_slice(window, (k // 8 * NB, 0), (3 * NB, NB)).astype(BF16)
    partner = lax.ppermute(own, "prow", core_swap())
    partner, others = lax.optimization_barrier((partner, others))
    messages = pair_up(window, c, along, others, (1, 2, 3))
    messages, own, partner, others, keep_scalars = lax.optimization_barrier((messages, own, partner, others, scalars))
    messages = pair_up(window, c, along, others, (0,)) + messages

    moved = stage(messages, 0, ORDER[0])
    pair = side_by_side(own, partner, c)
    got = send_rows(own, pair)
    out = keep_column(keep_scalars, window)
    moved, got, out = lax.optimization_barrier((moved, got, out))
    message = take(d_along, moved, ORDER[0])

    message, got = lax.optimization_barrier((message, got))

    tiles = over_rows(pair, got, c)
    look = k + jnp.arange(LOOK + 1)
    at = (x - look % 8 // 2) % 4 * 6 + look % 2 * 3 + look // 8 - k // 8
    places = jnp.concatenate([at, look[1:] % 16, jnp.reshape(c, (1,))])
    low, inv, weights = factor(places.astype(jnp.int32), tiles)
    late, weights = lax.optimization_barrier((message, weights))
    moved = stage([message, message, late, message], 1, ORDER[1])
    weights = lax.all_to_all(weights, "pcol", 0, 0, tiled=True)
    out = write_panel(scalars, window, low, inv, out)
    moved, weights, out = lax.optimization_barrier((moved, weights, out))
    message = pick(d_across, moved, ORDER[1])

    message, weights = lax.optimization_barrier((message, weights))
    mine = message[:PART]
    other = lax.ppermute(message[PART:], "prow", core_swap())
    first = stage([mine] * 4, 0, ORDER[2])
    second = stage([other] * 4, 1, ORDER[3])
    places = [4 * c + (along - s) % 4 for s in (0,) + ORDER[2]] + [4 * (1 - c) + (across - s) % 4 for s in (0,) + ORDER[3]]

    weights = lax.dynamic_slice(weights, (k * SHARE, 0), (SHARE, NB))
    weights = side_by_side(weights, lax.ppermute(weights, "prow", core_swap()), c)
    later = places[1:4] + places[5:]
    out, held = update(scalars, window, weights, [mine, other], places[::4], out, ahead=later)
    first, second, out, held = lax.optimization_barrier((first, second, out, held))
    return update(scalars, window, weights, first[1:] + second[1:], later, out, held=held)


def solution(mesh):
    return jax.shard_map(
        body,
        mesh=mesh,
        in_specs=(P("prow", "pcol"), P()),
        out_specs=P("prow", "pcol"),
        check_vma=False,
    )
```
